512 devices in a mesh: ctx: 64 (over z_hi, x, y, core), head: 8 (over z_lo).
Axes of the slice: x: 4, y: 4, z: 16 (z_hi: 2, z_lo: 8; z = z_hi * 8 + z_lo), core: 2. Of those that a mesh axis runs over, the one named last changes fastest.
Arguments:
- queries: bfloat16 [8192, 6144], P('ctx', 'head'), may hold values from -140 to 140
- keys: bfloat16 [8192, 6144], P('ctx', 'head'), may hold values from -5.05 to 5.05
- values: bfloat16 [8192, 6144], P('ctx', 'head'), may hold values from -6 to 6
- plan: int32 [2, 64], replicated, may hold values from 0 to 63, as said below
- w_out: bfloat16 [6144, 6144], P('head', 'ctx'), may hold values from -3.5 to 3.5
Outputs:
- projected: bfloat16 [8192, 6144], P('ctx', 'head')
The draws below stay inside these ranges and needn't reach their ends.
Inputs may be any that keep to these rules, and one draw needn't show every extreme that they name: plan comes from the circle method over 64 blocks: each row is a pairing, plan[r, plan[r, b]] = b and plan[r, b] != b, and the rounds give each block different partners.
All inputs are finite; a program needn't handle non-finite values.
Results may differ from the reference program's by a relative error of at most 0.017.
Values may be sent and summed in bfloat16 or wider, within the bound.
No kernel may reach another device: no remote copies, remote signals or barrier semaphores. Data moves between devices by JAX's collectives and lax.ppermute only.
A program may use at most 64 MiB of HBM per device.

```python
import jax
import jax.numpy as jnp
from jax import lax

HEADS = 48
HEAD_DIM = 128
D = 6144
BLOCK = 128
ROUNDS = 2
BLOCKS = 64
TOKENS = 8192
N_HEAD = 8


def keys_base(key):
    return jnp.clip(jax.random.normal(key, (TOKENS, HEADS * HEAD_DIM), jnp.float32), -5.0, 5.0)


def draw_keys(key, part):
    base = keys_base(key)
    return base.astype(jnp.bfloat16)


def draw_queries(key, part):
    key = jax.random.fold_in(key, 7)
    fresh = jnp.clip(jax.random.normal(key, (TOKENS, HEADS * HEAD_DIM), jnp.float32), -5.0, 5.0)
    return fresh.astype(jnp.bfloat16)


def draw_plan(key, part):
    key = jax.random.fold_in(key, 3)
    seat_key, turn_key = jax.random.split(key)
    seats = jax.random.permutation(seat_key, BLOCKS).astype(jnp.int32)
    block_at = jnp.zeros((BLOCKS,), jnp.int32).at[seats].set(jnp.arange(BLOCKS, dtype=jnp.int32))
    picks = jax.random.permutation(turn_key, BLOCKS - 1)[:ROUNDS].astype(jnp.int32)
    circle = BLOCKS - 1

    def one_turn(pick):
        other = jnp.where(seats == circle, pick, jnp.where(seats == pick, circle, (2 * pick - seats) % circle))
        return block_at[other]
    return jax.vmap(one_turn)(picks).astype(jnp.int32)


def with_spikes(array, own_key, source, target, shards_of, factor):
    def block_of(dim):
        return (jnp.arange(array.shape[dim]) // (array.shape[dim] // shards_of)).reshape((-1,) + (1,) * (array.ndim - 1 - dim))

    near = jax.random.permutation(own_key, shards_of)[block_of(target)]
    far = (block_of(target) + shards_of // 2) % shards_of
    return jnp.where((block_of(source) == near) | (block_of(source) == far), factor * array, array)


def block_scale(rng, shape, shards, least, high):
    factor_of = 1.0
    for axis_at, shards_of in shards:
        draws = jax.random.uniform(jax.random.fold_in(jax.random.fold_in(rng, 6), axis_at), (shards_of,), jnp.float32, least / len(shards), high / len(shards))
        factor_of = factor_of * jnp.repeat(jnp.exp(draws), shape[axis_at] // shards_of).reshape((-1,) + (1,) * (len(shape) - 1 - axis_at))
    return factor_of


def scatter_about(key, shape, scale, bound, shards=(), kind=jnp.bfloat16):
    factor_of = block_scale(key, shape, shards, -0.22, 0.18) if shards else 1.0
    entries = jax.random.normal(key, shape, jnp.float32) * scale * factor_of
    return jnp.minimum(jnp.maximum(entries, -bound), bound).astype(kind)


def noise_with(key, dims, spread, bound, cuts, heavy, kind=jnp.bfloat16):
    values = spread * jax.random.normal(key, dims, jnp.float32)
    if cuts:
        values = values * block_scale(key, dims, cuts, -0.22, 0.18)
    return jnp.clip(with_spikes(values, jax.random.fold_in(key, 3), *heavy), -bound, bound).astype(kind)


def setup_inputs(seed: int = 0) -> dict:
    seeds = jax.random.split(jax.random.key(seed), 6)
    queries = draw_queries(jax.random.fold_in(seeds[5], 71), 0)
    keys = draw_keys(jax.random.fold_in(seeds[5], 71), 0)
    values = scatter_about(seeds[2], (TOKENS, HEADS * HEAD_DIM), 1.0, 6.0, ((0, 64), (1, 8)))
    plan = draw_plan(jax.random.fold_in(seeds[5], 71), 0)
    w_out = noise_with(seeds[4], (HEADS * HEAD_DIM, D), 0.2, 3.5, ((0, 8), (1, 64)), (0, 1, 64, 4.0))
    return {"queries": queries, "keys": keys, "values": values, "plan": plan, "w_out": w_out}


def reference(queries, keys, values, plan, w_out):
    inner_width = HEADS * HEAD_DIM
    score_scale = 1.0 / (HEAD_DIM ** 0.5)
    query_blocks = queries.reshape(BLOCKS, BLOCK, HEADS, HEAD_DIM)
    key_blocks = keys.reshape(BLOCKS, BLOCK, HEADS, HEAD_DIM)
    value_blocks = values.reshape(BLOCKS, BLOCK, HEADS, HEAD_DIM)

    def attend(block_id):
        chosen = [block_id] + [plan[turn_index, block_id] for turn_index in range(ROUNDS)]
        key_rows = jnp.concatenate([key_blocks[which] for which in chosen], 0).astype(jnp.float32)
        value_rows = jnp.concatenate([value_blocks[which] for which in chosen], 0).astype(jnp.float32)
        query_rows = query_blocks[block_id].astype(jnp.float32)
        scores = jnp.einsum("qhd,khd->hqk", query_rows, key_rows) * score_scale
        row_peak = jnp.max(scores, axis=-1, keepdims=True)
        exponent = jnp.exp(scores - row_peak)
        row_total = jnp.sum(exponent, axis=-1)
        weights = exponent.astype(jnp.bfloat16).astype(jnp.float32)
        summed = jnp.einsum("hqk,khd->qhd", weights, value_rows)
        return (summed / jnp.transpose(row_total)[:, :, None]).astype(jnp.bfloat16)

    attended = lax.map(attend, jnp.arange(BLOCKS, dtype=jnp.int32)).reshape(TOKENS, inner_width)
    group_cols = inner_width // N_HEAD
    summed_out = jnp.zeros((TOKENS, D), jnp.float32)
    for group_id in range(N_HEAD):
        lower = group_id * group_cols
        partial_term = jnp.dot(attended[:, lower:lower + group_cols], w_out[lower:lower + group_cols], preferred_element_type=jnp.float32).astype(jnp.bfloat16)
        partial_term = lax.optimization_barrier(partial_term)
        summed_out = summed_out + partial_term.astype(jnp.float32)
    return summed_out.astype(jnp.bfloat16)
```

```python
import jax
import jax.numpy as jnp
from jax import lax
from jax.experimental import pallas as pl
from jax.experimental.pallas import tpu as pltpu
from jax.sharding import Mesh, PartitionSpec as P

HEAD_DIM = 128
ROUNDS = 2
SIZES = (2, 4, 4, 2, 2, 4)
NAMES = ("zh", "x", "y", "c", "p", "q")
CTX = ("zh", "x", "y", "c")
HEAD = ("p", "q")
PLANE = ("x", "y", "c")
SWAP = ((0, 1), (1, 0))
QUAD = 4
PIECE = 8


def exchange_x_q(flip):
    place = lambda zh, x, q: (zh * QUAD + x) * QUAD + q
    return [
        (place(zh, x, q), place(zh ^ flip, q, x))
        for zh in range(2)
        for x in range(QUAD)
        for q in range(QUAD)
    ]


def project_kernel(order_ref, *refs):
    parts, (w_ref, out_ref, total) = refs[:QUAD], refs[QUAD:]
    step = pl.program_id(0)
    width = w_ref.shape[-1]

    @pl.when(step == 0)
    def _():
        total[...] = jnp.zeros_like(total)

    rows = w_ref[...].reshape(-1, width)
    for at, part in enumerate(parts):

        @pl.when(step == at)
        def _(part=part):
            total[...] += lax.dot_general(
                part[...], rows, (((1,), (1,)), ((), ())), preferred_element_type=jnp.float32
            )

    @pl.when(step == QUAD - 1)
    def _():
        out_ref[...] = total[...].astype(out_ref.dtype)


def project(order, parts, w_all, side, dtype):
    tokens, width = parts[0].shape
    _, chunks, _, columns, _ = w_all.shape
    whole = pl.BlockSpec((tokens, width), lambda k, order: (0, 0))
    return pl.pallas_call(
        project_kernel,
        grid_spec=pltpu.PrefetchScalarGridSpec(
            num_scalar_prefetch=1,
            grid=(QUAD,),
            in_specs=[whole] * QUAD
            + [
                pl.BlockSpec(
                    (None, chunks, None, columns, width),
                    lambda k, order: (order[k], 0, side, 0, 0),
                )
            ],
            out_specs=pl.BlockSpec((tokens, chunks * columns), lambda k, order: (0, 0)),
            scratch_shapes=[pltpu.VMEM((tokens, chunks * columns), jnp.float32)],
        ),
        out_shape=jax.ShapeDtypeStruct((tokens, chunks * columns), dtype),
        compiler_params=pltpu.CompilerParams(
            dimension_semantics=("arbitrary",), vmem_limit_bytes=32 << 20
        ),
        cost_estimate=pl.CostEstimate(
            flops=2 * QUAD * tokens * width * chunks * columns,
            bytes_accessed=2 * QUAD * width * (chunks * columns + tokens),
            transcendentals=0,
        ),
    )(order, *parts, w_all)


def body(queries, keys, values, plan, w_out):
    tokens, width = queries.shape
    heads = width // HEAD_DIM
    half = lax.axis_index("zh")
    quad, member = lax.axis_index("p"), lax.axis_index("q")
    seats = lax.axis_size(PLANE)
    pieces = tokens // PIECE

    own = jnp.stack((keys, values)).reshape(2 * pieces, PIECE, width)
    far = lax.ppermute(own, "zh", SWAP)

    w_rows = w_out.T
    w_near = lax.ppermute(w_rows, ("zh", "x", "q"), exchange_x_q(0))
    w_far = lax.ppermute(w_rows, ("zh", "x", "q"), exchange_x_q(1))
    keeps_near = half == quad
    w_pair = jnp.stack(
        (jnp.where(keeps_near, w_near, w_far), jnp.where(keeps_near, w_far, w_near))
    )
    w_all = lax.all_gather(w_pair, PLANE, axis=0, tiled=False)
    w_all = w_all.reshape(QUAD, seats // QUAD, 2, -1, width)

    both = jnp.stack((own, far), 1)
    spread = lax.all_to_all(both, PLANE, split_axis=0, concat_axis=0, tiled=True)
    spread = spread.reshape(2 * seats, PIECE, width)
    wanted = lax.dynamic_slice_in_dim(plan, half * seats, seats, 1)
    place = (wanted % seats) * 2 + (wanted // seats ^ half)
    chosen = spread.at[place.T].get(mode="promise_in_bounds")
    routed = lax.all_to_all(chosen, PLANE, split_axis=0, concat_axis=0, tiled=True)
    routed = routed.reshape(2, pieces, ROUNDS, PIECE, width).transpose(0, 2, 1, 3, 4)
    routed = routed.reshape(2, ROUNDS * tokens, width)

    key_rows = jnp.concatenate((keys, routed[0])).reshape(-1, heads, HEAD_DIM)
    value_rows = jnp.concatenate((values, routed[1])).reshape(-1, heads, HEAD_DIM)
    query_rows = queries.reshape(tokens, heads, HEAD_DIM)
    scores = jnp.einsum(
        "qhd,khd->hqk", query_rows, key_rows, preferred_element_type=jnp.float32
    ) * (1.0 / HEAD_DIM**0.5)
    exponent = jnp.exp(scores - jnp.max(scores, axis=-1, keepdims=True))
    row_total = jnp.sum(exponent, axis=-1)
    summed = jnp.einsum(
        "hqk,khd->qhd",
        exponent.astype(jnp.bfloat16),
        value_rows,
        preferred_element_type=jnp.float32,
    )
    attended = (summed / row_total.T[:, :, None]).astype(jnp.bfloat16).reshape(tokens, width)

    parts = [attended] + [
        lax.ppermute(attended, "q", [(i, i ^ k) for i in range(QUAD)]) for k in range(1, QUAD)
    ]
    order = member ^ jnp.arange(QUAD, dtype=jnp.int32)
    sent = project(order, parts, w_all, 1, jnp.bfloat16)
    arrived = lax.ppermute(sent, "p", SWAP)
    kept = project(order, parts, w_all, 0, jnp.float32)
    return (kept + arrived.astype(jnp.float32)).astype(jnp.bfloat16)


def solution(mesh):
    fine = Mesh(mesh.devices.reshape(SIZES), NAMES)
    return jax.shard_map(
        body,
        mesh=fine,
        in_specs=(P(CTX, HEAD), P(CTX, HEAD), P(CTX, HEAD), P(), P(HEAD, CTX)),
        out_specs=P(CTX, HEAD),
        check_vma=False,
    )
```

```python
import jax
import jax.numpy as jnp
from jax import lax
from jax.experimental import pallas as pl
from jax.experimental.pallas import tpu as pltpu
from jax.sharding import Mesh, PartitionSpec as P

HEAD_DIM = 128
ROUNDS = 2
SIZES = (2, 4, 4, 2, 2, 4)
NAMES = ("zh", "x", "y", "c", "p", "q")
CTX = ("zh", "x", "y", "c")
HEAD = ("p", "q")
PLANE = ("x", "y", "c")
SWAP = ((0, 1), (1, 0))
QUAD = 4
PIECE = 8


def exchange_x_q(flip):
    place = lambda zh, x, q: (zh * QUAD + x) * QUAD + q
    return [
        (place(zh, x, q), place(zh ^ flip, q, x))
        for zh in range(2)
        for x in range(QUAD)
        for q in range(QUAD)
    ]


def project_kernel(order_ref, *refs):
    parts, (w_ref, out_ref, total) = refs[:QUAD], refs[QUAD:]
    step = pl.program_id(0)
    width = w_ref.shape[-1]

    @pl.when(step == 0)
    def _():
        total[...] = jnp.zeros_like(total)

    rows = w_ref[...].reshape(-1, width)
    for at, part in enumerate(parts):

        @pl.when(step == at)
        def _(part=part):
            total[...] += lax.dot_general(
                part[...], rows, (((1,), (1,)), ((), ())), preferred_element_type=jnp.float32
            )

    @pl.when(step == QUAD - 1)
    def _():
        out_ref[...] = total[...].astype(out_ref.dtype)


def project(order, parts, w_all, side, dtype):
    tokens, width = parts[0].shape
    _, chunks, _, columns, _ = w_all.shape
    whole = pl.BlockSpec((tokens, width), lambda k, order: (0, 0))
    return pl.pallas_call(
        project_kernel,
        grid_spec=pltpu.PrefetchScalarGridSpec(
            num_scalar_prefetch=1,
            grid=(QUAD,),
            in_specs=[whole] * QUAD
            + [
                pl.BlockSpec(
                    (None, chunks, None, columns, width),
                    lambda k, order: (order[k], 0, side, 0, 0),
                )
            ],
            out_specs=pl.BlockSpec((tokens, chunks * columns), lambda k, order: (0, 0)),
            scratch_shapes=[pltpu.VMEM((tokens, chunks * columns), jnp.float32)],
        ),
        out_shape=jax.ShapeDtypeStruct((tokens, chunks * columns), dtype),
        compiler_params=pltpu.CompilerParams(
            dimension_semantics=("arbitrary",), vmem_limit_bytes=56 << 20
        ),
        cost_estimate=pl.CostEstimate(
            flops=2 * QUAD * tokens * width * chunks * columns,
            bytes_accessed=2 * QUAD * width * (chunks * columns + tokens),
            transcendentals=0,
        ),
    )(order, *parts, w_all)


def body(queries, keys, values, plan, w_out):
    tokens, width = queries.shape
    heads = width // HEAD_DIM
    half = lax.axis_index("zh")
    quad, member = lax.axis_index("p"), lax.axis_index("q")
    seats = lax.axis_size(PLANE)
    pieces = tokens // PIECE

    w_rows = w_out.T
    w_near = lax.ppermute(w_rows, ("zh", "x", "q"), exchange_x_q(0))
    w_far = lax.ppermute(w_rows, ("zh", "x", "q"), exchange_x_q(1))
    keeps_near = half == quad
    w_pair = jnp.stack(
        (jnp.where(keeps_near, w_near, w_far), jnp.where(keeps_near, w_far, w_near))
    )

    own = jnp.stack((keys, values)).reshape(2 * pieces, PIECE, width)
    spread = lax.all_to_all(own, PLANE, split_axis=0, concat_axis=0, tiled=True)
    spread, w_pair = lax.optimization_barrier((spread, w_pair))
    far = lax.ppermute(spread, "zh", SWAP)

    w_all = lax.all_gather(w_pair, PLANE, axis=0, tiled=False)
    w_all = w_all.reshape(QUAD, seats // QUAD, 2, -1, width)

    wanted = lax.dynamic_slice_in_dim(plan, half * seats, seats, 1)
    place = (wanted // seats ^ half) * seats + wanted % seats
    chosen = jnp.concatenate((spread, far)).at[place.T].get(mode="promise_in_bounds")
    routed = lax.all_to_all(chosen, PLANE, split_axis=0, concat_axis=0, tiled=True)
    routed = routed.reshape(2, pieces, ROUNDS, PIECE, width).transpose(0, 2, 1, 3, 4)
    routed = routed.reshape(2, ROUNDS * tokens, width)

    key_rows = jnp.concatenate((keys, routed[0])).reshape(-1, heads, HEAD_DIM)
    value_rows = jnp.concatenate((values, routed[1])).reshape(-1, heads, HEAD_DIM)
    query_rows = queries.reshape(tokens, heads, HEAD_DIM)
    scores = jnp.einsum(
        "qhd,khd->hqk", query_rows, key_rows, preferred_element_type=jnp.float32
    ) * (1.0 / HEAD_DIM**0.5)
    exponent = jnp.exp(scores - jnp.max(scores, axis=-1, keepdims=True))
    row_total = jnp.sum(exponent, axis=-1)
    summed = jnp.einsum(
        "hqk,khd->qhd",
        exponent.astype(jnp.bfloat16),
        value_rows,
        preferred_element_type=jnp.float32,
    )
    attended = (summed / row_total.T[:, :, None]).astype(jnp.bfloat16).reshape(tokens, width)

    parts = [attended] + [
        lax.ppermute(attended, "q", [(i, i ^ k) for i in range(QUAD)]) for k in range(1, QUAD)
    ]
    order = member ^ jnp.arange(QUAD, dtype=jnp.int32)
    sent = project(order, parts, w_all, 1, jnp.bfloat16)
    arrived = lax.ppermute(sent, "p", SWAP)
    kept = project(order, parts, w_all, 0, jnp.float32)
    return (kept + arrived.astype(jnp.float32)).astype(jnp.bfloat16)


def solution(mesh):
    fine = Mesh(mesh.devices.reshape(SIZES), NAMES)
    return jax.shard_map(
        body,
        mesh=fine,
        in_specs=(P(CTX, HEAD), P(CTX, HEAD), P(CTX, HEAD), P(), P(HEAD, CTX)),
        out_specs=P(CTX, HEAD),
        check_vma=False,
    )
```

```python
import functools

import jax
import jax.numpy as jnp
from jax import lax
from jax.experimental import pallas as pl
from jax.experimental.pallas import tpu as pltpu
from jax.sharding import Mesh, PartitionSpec as P

HEAD_DIM = 128
ROUNDS = 2
SIZES = (2, 4, 4, 2, 2, 4)
NAMES = ("zh", "x", "y", "c", "p", "q")
CTX = ("zh", "x", "y", "c")
HEAD = ("p", "q")
PLANE = ("x", "y", "c")
SWAP = ((0, 1), (1, 0))
QUAD = 4
PIECE = 8


def project_kernel(order_ref, *refs, side):
    parts, (w_ref, out_ref, held, arrivals) = refs[:QUAD], refs[QUAD:]
    width = w_ref.shape[-1]
    copies = [
        pltpu.make_async_copy(w_ref.at[order_ref[k], :, side], held.at[k], arrivals.at[k])
        for k in range(QUAD)
    ]
    for copy in copies:
        copy.start()
    total = 0.0
    for k in range(QUAD):
        copies[k].wait()
        total += lax.dot_general(
            parts[k][...],
            held[k].reshape(-1, width),
            (((1,), (1,)), ((), ())),
            preferred_element_type=jnp.float32,
        )
    out_ref[...] = total.astype(out_ref.dtype)


def project(order, parts, w_all, side, dtype):
    tokens, width = parts[0].shape
    _, chunks, _, columns, _ = w_all.shape
    in_vmem = pl.BlockSpec(memory_space=pltpu.VMEM)
    return pl.pallas_call(
        functools.partial(project_kernel, side=side),
        in_specs=[pl.BlockSpec(memory_space=pltpu.SMEM)]
        + [in_vmem] * QUAD
        + [pl.BlockSpec(memory_space=pltpu.HBM)],
        out_specs=in_vmem,
        out_shape=jax.ShapeDtypeStruct((tokens, chunks * columns), dtype),
        scratch_shapes=[
            pltpu.VMEM((QUAD, chunks, columns, width), w_all.dtype),
            pltpu.SemaphoreType.DMA((QUAD,)),
        ],
        compiler_params=pltpu.CompilerParams(vmem_limit_bytes=32 << 20),
        cost_estimate=pl.CostEstimate(
            flops=2 * QUAD * tokens * width * chunks * columns,
            bytes_accessed=2 * QUAD * width * (chunks * columns + tokens),
            transcendentals=0,
        ),
    )(order, *parts, pltpu.with_memory_space_constraint(w_all, pltpu.HBM))


def body(queries, keys, values, plan, w_out):
    tokens, width = queries.shape
    heads = width // HEAD_DIM
    half = lax.axis_index("zh")
    quad, member = lax.axis_index("p"), lax.axis_index("q")
    seats = lax.axis_size(PLANE)
    pieces = tokens // PIECE

    w_near = lax.ppermute(
        w_out.T,
        ("x", "q"),
        [(x * QUAD + q, q * QUAD + x) for x in range(QUAD) for q in range(QUAD)],
    )
    w_far = lax.ppermute(w_near, "zh", SWAP)
    keeps_near = half == quad
    w_pair = jnp.stack(
        (jnp.where(keeps_near, w_near, w_far), jnp.where(keeps_near, w_far, w_near))
    )

    own = jnp.stack((keys, values)).reshape(2 * pieces, PIECE, width)
    spread = lax.all_to_all(own, PLANE, split_axis=0, concat_axis=0, tiled=True)
    spread, w_pair = lax.optimization_barrier((spread, w_pair))
    far = lax.ppermute(spread, "zh", SWAP)

    w_all = lax.all_gather(w_pair, PLANE, axis=0, tiled=False)
    w_all = w_all.reshape(QUAD, seats // QUAD, 2, -1, width)

    wanted = lax.dynamic_slice_in_dim(plan, half * seats, seats, 1)
    place = (wanted // seats ^ half) * seats + wanted % seats
    chosen = jnp.concatenate((spread, far)).at[place.T].get(mode="promise_in_bounds")
    routed = lax.all_to_all(chosen, PLANE, split_axis=0, concat_axis=0, tiled=True)
    routed = routed.reshape(2, pieces, ROUNDS, PIECE, width).transpose(0, 2, 1, 3, 4)
    routed = routed.reshape(2, ROUNDS * tokens, width)

    key_rows = jnp.concatenate((keys, routed[0])).reshape(-1, heads, HEAD_DIM)
    value_rows = jnp.concatenate((values, routed[1])).reshape(-1, heads, HEAD_DIM)
    query_rows = queries.reshape(tokens, heads, HEAD_DIM)
    scores = jnp.einsum(
        "qhd,khd->hqk", query_rows, key_rows, preferred_element_type=jnp.float32
    ) * (1.0 / HEAD_DIM**0.5)
    exponent = jnp.exp(scores - jnp.max(scores, axis=-1, keepdims=True))
    row_total = jnp.sum(exponent, axis=-1)
    summed = jnp.einsum(
        "hqk,khd->qhd",
        exponent.astype(jnp.bfloat16),
        value_rows,
        preferred_element_type=jnp.float32,
    )
    attended = (summed / row_total.T[:, :, None]).astype(jnp.bfloat16).reshape(tokens, width)

    parts = [attended] + [
        lax.ppermute(attended, "q", [(i, i ^ k) for i in range(QUAD)]) for k in range(1, QUAD)
    ]
    order = member ^ jnp.arange(QUAD, dtype=jnp.int32)
    sent = project(order, parts, w_all, 1, jnp.bfloat16)
    arrived = lax.ppermute(sent, "p", SWAP)
    kept = project(order, parts, w_all, 0, jnp.float32)
    return (kept + arrived.astype(jnp.float32)).astype(jnp.bfloat16)


def solution(mesh):
    fine = Mesh(mesh.devices.reshape(SIZES), NAMES)
    return jax.shard_map(
        body,
        mesh=fine,
        in_specs=(P(CTX, HEAD), P(CTX, HEAD), P(CTX, HEAD), P(), P(HEAD, CTX)),
        out_specs=P(CTX, HEAD),
        check_vma=False,
    )
```

```python
import functools

import jax
import jax.numpy as jnp
from jax import lax
from jax.experimental import pallas as pl
from jax.experimental.pallas import tpu as pltpu
from jax.sharding import Mesh, PartitionSpec as P

HEAD_DIM = 128
ROUNDS = 2
SIZES = (2, 4, 4, 2, 2, 4)
NAMES = ("zh", "x", "y", "c", "p", "q")
CTX = ("zh", "x", "y", "c")
HEAD = ("p", "q")
PLANE = ("x", "y", "c")
SWAP = ((0, 1), (1, 0))
QUAD = 4
HALVES = 2
PIECE = 8


def project_kernel(order_ref, *refs, side):
    parts, (w_ref, out_ref, held, arrivals) = refs[: HALVES * QUAD], refs[HALVES * QUAD :]
    width = w_ref.shape[-1]
    copies = [
        pltpu.make_async_copy(w_ref.at[order_ref[k], :, side], held.at[k], arrivals.at[k])
        for k in range(QUAD)
    ]
    for copy in copies:
        copy.start()
    total = 0.0
    for k in range(QUAD):
        copies[k].wait()
        rows = held[k].reshape(-1, width)
        for half in range(HALVES):
            total += lax.dot_general(
                parts[half * QUAD + k][...],
                rows[:, half * width // HALVES : (half + 1) * width // HALVES],
                (((1,), (1,)), ((), ())),
                preferred_element_type=jnp.float32,
            )
    out_ref[...] = total.astype(out_ref.dtype)


def project(order, parts, w_all, side, dtype):
    tokens = parts[0].shape[0]
    _, chunks, _, columns, width = w_all.shape
    in_vmem = pl.BlockSpec(memory_space=pltpu.VMEM)
    return pl.pallas_call(
        functools.partial(project_kernel, side=side),
        in_specs=[pl.BlockSpec(memory_space=pltpu.SMEM)]
        + [in_vmem] * len(parts)
        + [pl.BlockSpec(memory_space=pltpu.HBM)],
        out_specs=in_vmem,
        out_shape=jax.ShapeDtypeStruct((tokens, chunks * columns), dtype),
        scratch_shapes=[
            pltpu.VMEM((QUAD, chunks, columns, width), w_all.dtype),
            pltpu.SemaphoreType.DMA((QUAD,)),
        ],
        compiler_params=pltpu.CompilerParams(vmem_limit_bytes=32 << 20),
        cost_estimate=pl.CostEstimate(
            flops=2 * QUAD * tokens * width * chunks * columns,
            bytes_accessed=2 * QUAD * width * (chunks * columns + tokens),
            transcendentals=0,
        ),
    )(order, *parts, pltpu.with_memory_space_constraint(w_all, pltpu.HBM))


def attend(query_cols, key_cols, value_cols):
    tokens, width = query_cols.shape
    split = lambda cols: cols.reshape(-1, width // HEAD_DIM, HEAD_DIM)
    scores = jnp.einsum(
        "qhd,khd->hqk", split(query_cols), split(key_cols), preferred_element_type=jnp.float32
    ) * (1.0 / HEAD_DIM**0.5)
    exponent = jnp.exp(scores - jnp.max(scores, axis=-1, keepdims=True))
    row_total = jnp.sum(exponent, axis=-1)
    summed = jnp.einsum(
        "hqk,khd->qhd",
        exponent.astype(jnp.bfloat16),
        split(value_cols),
        preferred_element_type=jnp.float32,
    )
    return (summed / row_total.T[:, :, None]).astype(jnp.bfloat16).reshape(tokens, width)


def body(queries, keys, values, plan, w_out):
    tokens, width = queries.shape
    half = lax.axis_index("zh")
    quad, member = lax.axis_index("p"), lax.axis_index("q")
    seats = lax.axis_size(PLANE)
    pieces = tokens // PIECE
    part = width // HALVES
    cut = lambda cols, h: cols[:, h * part : (h + 1) * part]
    plane_swap = lambda sent: lax.all_to_all(sent, PLANE, split_axis=0, concat_axis=0, tiled=True)

    w_near = lax.ppermute(
        w_out.T,
        ("x", "q"),
        [(x * QUAD + q, q * QUAD + x) for x in range(QUAD) for q in range(QUAD)],
    )

    spread = [
        plane_swap(
            jnp.stack((cut(keys, h), cut(values, h))).reshape(2 * pieces, PIECE, part)
        )
        for h in range(HALVES)
    ]
    w_near, spread[0] = lax.optimization_barrier((w_near, spread[0]))
    w_far = lax.ppermute(w_near, "zh", SWAP)
    keeps_near = half == quad
    w_pair = jnp.stack(
        (jnp.where(keeps_near, w_near, w_far), jnp.where(keeps_near, w_far, w_near))
    )
    w_pair, spread[1] = lax.optimization_barrier((w_pair, spread[1]))
    w_all = lax.all_gather(w_pair, PLANE, axis=0, tiled=False)
    w_all = w_all.reshape(QUAD, seats // QUAD, 2, -1, width)

    wanted = lax.dynamic_slice_in_dim(plan, half * seats, seats, 1)
    place = ((wanted // seats ^ half) * seats + wanted % seats).T
    parts = []
    for h in range(HALVES):
        far = lax.ppermute(spread[h], "zh", SWAP)
        chosen = jnp.concatenate((spread[h], far)).at[place].get(mode="promise_in_bounds")
        routed = plane_swap(chosen)
        routed = routed.reshape(2, pieces, ROUNDS, PIECE, part).transpose(0, 2, 1, 3, 4)
        routed = routed.reshape(2, ROUNDS * tokens, part)
        attended = attend(
            cut(queries, h),
            jnp.concatenate((cut(keys, h), routed[0])),
            jnp.concatenate((cut(values, h), routed[1])),
        )
        parts += [attended] + [
            lax.ppermute(attended, "q", [(i, i ^ k) for i in range(QUAD)])
            for k in range(1, QUAD)
        ]

    order = member ^ jnp.arange(QUAD, dtype=jnp.int32)
    sent = project(order, parts, w_all, 1, jnp.bfloat16)
    arrived = lax.ppermute(sent, "p", SWAP)
    kept = project(order, parts, w_all, 0, jnp.float32)
    return (kept + arrived.astype(jnp.float32)).astype(jnp.bfloat16)


def solution(mesh):
    fine = Mesh(mesh.devices.reshape(SIZES), NAMES)
    return jax.shard_map(
        body,
        mesh=fine,
        in_specs=(P(CTX, HEAD), P(CTX, HEAD), P(CTX, HEAD), P(), P(HEAD, CTX)),
        out_specs=P(CTX, HEAD),
        check_vma=False,
    )
```

```python
import functools

import jax
import jax.numpy as jnp
from jax import lax
from jax.experimental import pallas as pl
from jax.experimental.pallas import tpu as pltpu
from jax.sharding import Mesh, PartitionSpec as P

HEAD_DIM = 128
ROUNDS = 2
SIZES = (2, 4, 4, 2, 2, 4)
NAMES = ("zh", "x", "y", "c", "p", "q")
CTX = ("zh", "x", "y", "c")
HEAD = ("p", "q")
PLANE = ("x", "y", "c")
SWAP = ((0, 1), (1, 0))
QUAD = 4
HINT_FLOPS, HINT_BYTES = 170 * 10**9, 10**6
HALVES = 2
PIECE = 16


def project_kernel(order_ref, *refs, side):
    parts, (w_ref, out_ref, held, arrivals) = refs[:QUAD], refs[QUAD:]
    width = w_ref.shape[-1]
    copies = [
        pltpu.make_async_copy(w_ref.at[order_ref[k], :, side], held.at[k], arrivals.at[k])
        for k in range(QUAD)
    ]
    for copy in copies:
        copy.start()
    total = 0.0
    for k in range(QUAD):
        copies[k].wait()
        total += lax.dot_general(
            parts[k][...],
            held[k].reshape(-1, width),
            (((1,), (1,)), ((), ())),
            preferred_element_type=jnp.float32,
        )
    out_ref[...] = total.astype(out_ref.dtype)


def project(order, parts, w_all, side, dtype):
    tokens, width = parts[0].shape
    _, chunks, _, columns, _ = w_all.shape
    in_vmem = pl.BlockSpec(memory_space=pltpu.VMEM)
    return pl.pallas_call(
        functools.partial(project_kernel, side=side),
        in_specs=[pl.BlockSpec(memory_space=pltpu.SMEM)]
        + [in_vmem] * QUAD
        + [pl.BlockSpec(memory_space=pltpu.HBM)],
        out_specs=in_vmem,
        out_shape=jax.ShapeDtypeStruct((tokens, chunks * columns), dtype),
        scratch_shapes=[
            pltpu.VMEM((QUAD, chunks, columns, width), w_all.dtype),
            pltpu.SemaphoreType.DMA((QUAD,)),
        ],
        compiler_params=pltpu.CompilerParams(vmem_limit_bytes=32 << 20),
        cost_estimate=pl.CostEstimate(
            flops=2 * QUAD * tokens * width * chunks * columns,
            bytes_accessed=2 * QUAD * width * (chunks * columns + tokens),
            transcendentals=0,
        ),
    )(order, *parts, pltpu.with_memory_space_constraint(w_all, pltpu.HBM))


def attend_kernel(q_ref, k_ref, v_ref, routed_ref, out_ref):
    tokens, width = q_ref.shape
    part = width // HALVES
    for head in range(width // HEAD_DIM):
        cols = slice(head * HEAD_DIM, (head + 1) * HEAD_DIM)
        at, lane = divmod(head * HEAD_DIM, part)

        def rows(kind, turn):
            piece = routed_ref[kind * HALVES + at, :, turn, :, lane : lane + HEAD_DIM]
            return piece.reshape(tokens, HEAD_DIM)

        query = q_ref[:, cols]
        scores = [
            lax.dot_general(
                query, keys, (((1,), (1,)), ((), ())), preferred_element_type=jnp.float32
            )
            * (1.0 / HEAD_DIM**0.5)
            for keys in [k_ref[:, cols]] + [rows(0, turn) for turn in range(ROUNDS)]
        ]
        peak = functools.reduce(jnp.maximum, scores)
        peak = jnp.max(peak, axis=-1, keepdims=True)
        exponents = [jnp.exp(score - peak) for score in scores]
        row_total = jnp.sum(functools.reduce(jnp.add, exponents), axis=-1, keepdims=True)
        summed = 0.0
        for exponent, values in zip(
            exponents, [v_ref[:, cols]] + [rows(1, turn) for turn in range(ROUNDS)]
        ):
            summed += jnp.dot(
                exponent.astype(jnp.bfloat16), values, preferred_element_type=jnp.float32
            )
        out_ref[:, cols] = (summed / row_total).astype(out_ref.dtype)


def attend(queries, keys, values, routed):
    in_vmem = pl.BlockSpec(memory_space=pltpu.VMEM)
    return pl.pallas_call(
        attend_kernel,
        in_specs=[in_vmem] * 4,
        out_specs=in_vmem,
        out_shape=jax.ShapeDtypeStruct(queries.shape, queries.dtype),
        compiler_params=pltpu.CompilerParams(vmem_limit_bytes=32 << 20),
        cost_estimate=pl.CostEstimate(
            flops=HINT_FLOPS, bytes_accessed=HINT_BYTES, transcendentals=0
        ),
    )(queries, keys, values, routed)


def body(queries, keys, values, plan, w_out):
    tokens, width = queries.shape
    half = lax.axis_index("zh")
    quad, member = lax.axis_index("p"), lax.axis_index("q")
    seats = lax.axis_size(PLANE)

    w_near = lax.ppermute(
        w_out.T,
        ("x", "q"),
        [(x * QUAD + q, q * QUAD + x) for x in range(QUAD) for q in range(QUAD)],
    )
    w_far = lax.ppermute(w_near, "zh", SWAP)
    keeps_near = half == quad
    w_pair = jnp.stack(
        (jnp.where(keeps_near, w_near, w_far), jnp.where(keeps_near, w_far, w_near))
    )

    part = width // HALVES
    own = jnp.stack(
        [rows[:, h * part : (h + 1) * part] for rows in (keys, values) for h in range(HALVES)]
    )
    own = own.reshape(1, seats, PIECE, part)
    own = jnp.broadcast_to(own, (2, seats, PIECE, part)).reshape(2 * seats, PIECE, part)
    spread = lax.all_to_all(own, CTX, split_axis=0, concat_axis=0, tiled=True)
    spread, _ = lax.optimization_barrier((spread, w_pair))

    w_all = lax.all_gather(w_pair, PLANE, axis=0, tiled=False)
    w_all = w_all.reshape(QUAD, seats // QUAD, 2, -1, width)

    wanted = lax.dynamic_slice_in_dim(plan, half * seats, seats, 1)
    chosen = spread.at[wanted.T].get(mode="promise_in_bounds")
    routed = lax.all_to_all(chosen, PLANE, split_axis=0, concat_axis=0, tiled=True)
    attended = attend(
        queries,
        keys,
        values,
        routed.reshape(2 * HALVES, tokens // PIECE, ROUNDS, PIECE, part),
    )

    parts = [attended] + [
        lax.ppermute(attended, "q", [(i, i ^ k) for i in range(QUAD)]) for k in range(1, QUAD)
    ]
    order = member ^ jnp.arange(QUAD, dtype=jnp.int32)
    sent = project(order, parts, w_all, 1, jnp.bfloat16)
    arrived = lax.ppermute(sent, "p", SWAP)
    kept = project(order, parts, w_all, 0, jnp.float32)
    return (kept + arrived.astype(jnp.float32)).astype(jnp.bfloat16)


def solution(mesh):
    fine = Mesh(mesh.devices.reshape(SIZES), NAMES)
    return jax.shard_map(
        body,
        mesh=fine,
        in_specs=(P(CTX, HEAD), P(CTX, HEAD), P(CTX, HEAD), P(), P(HEAD, CTX)),
        out_specs=P(CTX, HEAD),
        check_vma=False,
    )
```

```python
import functools

import jax
import jax.numpy as jnp
from jax import lax
from jax.experimental import pallas as pl
from jax.experimental.pallas import tpu as pltpu
from jax.sharding import Mesh, PartitionSpec as P

HEAD_DIM = 128
ROUNDS = 2
SIZES = (2, 4, 4, 2, 2, 4)
NAMES = ("zh", "x", "y", "c", "p", "q")
CTX = ("zh", "x", "y", "c")
HEAD = ("p", "q")
PLANE = ("x", "y", "c")
SWAP = ((0, 1), (1, 0))
QUAD = 4
HINT_FLOPS, HINT_BYTES = 182 * 10**9, 10**6
HALVES = 2
PIECE = 16


def project_kernel(order_ref, *refs, side):
    parts, (w_ref, out_ref, held, arrivals) = refs[:QUAD], refs[QUAD:]
    width = w_ref.shape[-1]
    copies = [
        pltpu.make_async_copy(w_ref.at[order_ref[k], :, side], held.at[k], arrivals.at[k])
        for k in range(QUAD)
    ]
    for copy in copies:
        copy.start()
    total = 0.0
    for k in range(QUAD):
        copies[k].wait()
        total += lax.dot_general(
            parts[k][...],
            held[k].reshape(-1, width),
            (((1,), (1,)), ((), ())),
            preferred_element_type=jnp.float32,
        )
    out_ref[...] = total.astype(out_ref.dtype)


def project(order, parts, w_all, side, dtype):
    tokens, width = parts[0].shape
    _, chunks, _, columns, _ = w_all.shape
    in_vmem = pl.BlockSpec(memory_space=pltpu.VMEM)
    return pl.pallas_call(
        functools.partial(project_kernel, side=side),
        in_specs=[pl.BlockSpec(memory_space=pltpu.SMEM)]
        + [in_vmem] * QUAD
        + [pl.BlockSpec(memory_space=pltpu.HBM)],
        out_specs=in_vmem,
        out_shape=jax.ShapeDtypeStruct((tokens, chunks * columns), dtype),
        scratch_shapes=[
            pltpu.VMEM((QUAD, chunks, columns, width), w_all.dtype),
            pltpu.SemaphoreType.DMA((QUAD,)),
        ],
        compiler_params=pltpu.CompilerParams(vmem_limit_bytes=32 << 20),
        cost_estimate=pl.CostEstimate(
            flops=2 * QUAD * tokens * width * chunks * columns,
            bytes_accessed=2 * QUAD * width * (chunks * columns + tokens),
            transcendentals=0,
        ),
    )(order, *parts, pltpu.with_memory_space_constraint(w_all, pltpu.HBM))


def attend_kernel(q_ref, k_ref, v_ref, routed_ref, out_ref):
    tokens, width = q_ref.shape
    part = width // HALVES
    for head in range(width // HEAD_DIM):
        cols = slice(head * HEAD_DIM, (head + 1) * HEAD_DIM)
        at, lane = divmod(head * HEAD_DIM, part)

        def rows(kind, turn):
            piece = routed_ref[kind * HALVES + at, :, turn, :, lane : lane + HEAD_DIM]
            return piece.reshape(tokens, HEAD_DIM)

        query = q_ref[:, cols]
        scores = [
            lax.dot_general(
                query, keys, (((1,), (1,)), ((), ())), preferred_element_type=jnp.float32
            )
            * (1.0 / HEAD_DIM**0.5)
            for keys in [k_ref[:, cols]] + [rows(0, turn) for turn in range(ROUNDS)]
        ]
        peak = functools.reduce(jnp.maximum, scores)
        peak = jnp.max(peak, axis=-1, keepdims=True)
        exponents = [jnp.exp(score - peak) for score in scores]
        row_total = jnp.sum(functools.reduce(jnp.add, exponents), axis=-1, keepdims=True)
        summed = 0.0
        for exponent, values in zip(
            exponents, [v_ref[:, cols]] + [rows(1, turn) for turn in range(ROUNDS)]
        ):
            summed += jnp.dot(
                exponent.astype(jnp.bfloat16), values, preferred_element_type=jnp.float32
            )
        out_ref[:, cols] = (summed / row_total).astype(out_ref.dtype)


def attend(queries, keys, values, routed):
    in_vmem = pl.BlockSpec(memory_space=pltpu.VMEM)
    return pl.pallas_call(
        attend_kernel,
        in_specs=[in_vmem] * 4,
        out_specs=in_vmem,
        out_shape=jax.ShapeDtypeStruct(queries.shape, queries.dtype),
        compiler_params=pltpu.CompilerParams(vmem_limit_bytes=32 << 20),
        cost_estimate=pl.CostEstimate(
            flops=HINT_FLOPS, bytes_accessed=HINT_BYTES, transcendentals=0
        ),
    )(queries, keys, values, routed)


def body(queries, keys, values, plan, w_out):
    tokens, width = queries.shape
    half = lax.axis_index("zh")
    quad, member = lax.axis_index("p"), lax.axis_index("q")
    seats = lax.axis_size(PLANE)

    w_near = lax.ppermute(
        w_out.T,
        ("x", "q"),
        [(x * QUAD + q, q * QUAD + x) for x in range(QUAD) for q in range(QUAD)],
    )

    part = width // HALVES
    own = jnp.stack(
        [rows[:, h * part : (h + 1) * part] for rows in (keys, values) for h in range(HALVES)]
    )
    own = own.reshape(seats, PIECE, part)
    spread = lax.all_to_all(own, PLANE, split_axis=0, concat_axis=0, tiled=True)
    spread, w_near = lax.optimization_barrier((spread, w_near))

    w_far = lax.ppermute(w_near, "zh", SWAP)
    far = lax.ppermute(spread, "zh", SWAP)
    keeps_near = half == quad
    w_pair = jnp.stack(
        (jnp.where(keeps_near, w_near, w_far), jnp.where(keeps_near, w_far, w_near))
    )
    w_all = lax.all_gather(w_pair, PLANE, axis=0, tiled=False)
    w_all = w_all.reshape(QUAD, seats // QUAD, 2, -1, width)

    wanted = lax.dynamic_slice_in_dim(plan, half * seats, seats, 1)
    place = (wanted // seats ^ half) * seats + wanted % seats
    chosen = jnp.concatenate((spread, far)).at[place.T].get(mode="promise_in_bounds")
    routed = lax.all_to_all(chosen, PLANE, split_axis=0, concat_axis=0, tiled=True)
    attended = attend(
        queries,
        keys,
        values,
        routed.reshape(2 * HALVES, tokens // PIECE, ROUNDS, PIECE, part),
    )

    parts = [attended] + [
        lax.ppermute(attended, "q", [(i, i ^ k) for i in range(QUAD)]) for k in range(1, QUAD)
    ]
    order = member ^ jnp.arange(QUAD, dtype=jnp.int32)
    sent = project(order, parts, w_all, 1, jnp.bfloat16)
    arrived = lax.ppermute(sent, "p", SWAP)
    kept = project(order, parts, w_all, 0, jnp.float32)
    return (kept + arrived.astype(jnp.float32)).astype(jnp.bfloat16)


def solution(mesh):
    fine = Mesh(mesh.devices.reshape(SIZES), NAMES)
    return jax.shard_map(
        body,
        mesh=fine,
        in_specs=(P(CTX, HEAD), P(CTX, HEAD), P(CTX, HEAD), P(), P(HEAD, CTX)),
        out_specs=P(CTX, HEAD),
        check_vma=False,
    )
```

```python
import functools

import jax
import jax.numpy as jnp
from jax import lax
from jax.experimental import pallas as pl
from jax.experimental.pallas import tpu as pltpu
from jax.sharding import Mesh, PartitionSpec as P

HEAD_DIM = 128
ROUNDS = 2
SIZES = (2, 4, 4, 2, 2, 4)
NAMES = ("zh", "x", "y", "c", "p", "q")
CTX = ("zh", "x", "y", "c")
HEAD = ("p", "q")
PLANE = ("x", "y", "c")
SWAP = ((0, 1), (1, 0))
QUAD = 4
HINT_FLOPS, HINT_BYTES = 182 * 10**9, 10**6
HALVES = 2
PIECE = 16


def project_kernel(order_ref, *refs, side):
    parts, (w_ref, out_ref, held, arrivals) = refs[:QUAD], refs[QUAD:]
    width = w_ref.shape[-1]
    copies = [
        pltpu.make_async_copy(w_ref.at[order_ref[k], :, side], held.at[k], arrivals.at[k])
        for k in range(QUAD)
    ]
    for copy in copies:
        copy.start()
    total = 0.0
    for k in range(QUAD):
        copies[k].wait()
        total += lax.dot_general(
            parts[k][...],
            held[k].reshape(-1, width),
            (((1,), (1,)), ((), ())),
            preferred_element_type=jnp.float32,
        )
    out_ref[...] = total.astype(out_ref.dtype)


def project(order, parts, w_all, side, dtype):
    tokens, width = parts[0].shape
    _, chunks, _, columns, _ = w_all.shape
    in_vmem = pl.BlockSpec(memory_space=pltpu.VMEM)
    return pl.pallas_call(
        functools.partial(project_kernel, side=side),
        in_specs=[pl.BlockSpec(memory_space=pltpu.SMEM)]
        + [in_vmem] * QUAD
        + [pl.BlockSpec(memory_space=pltpu.HBM)],
        out_specs=in_vmem,
        out_shape=jax.ShapeDtypeStruct((tokens, chunks * columns), dtype),
        scratch_shapes=[
            pltpu.VMEM((QUAD, chunks, columns, width), w_all.dtype),
            pltpu.SemaphoreType.DMA((QUAD,)),
        ],
        compiler_params=pltpu.CompilerParams(vmem_limit_bytes=32 << 20),
        cost_estimate=pl.CostEstimate(
            flops=2 * QUAD * tokens * width * chunks * columns,
            bytes_accessed=2 * QUAD * width * (chunks * columns + tokens),
            transcendentals=0,
        ),
    )(order, *parts, pltpu.with_memory_space_constraint(w_all, pltpu.HBM))


def attend_kernel(q_ref, k_ref, v_ref, routed_ref, out_ref):
    tokens, width = q_ref.shape
    part = width // HALVES
    for head in range(width // HEAD_DIM):
        cols = slice(head * HEAD_DIM, (head + 1) * HEAD_DIM)
        at, lane = divmod(head * HEAD_DIM, part)

        def rows(kind, turn):
            piece = routed_ref[kind * HALVES + at, :, turn, :, lane : lane + HEAD_DIM]
            return piece.reshape(tokens, HEAD_DIM)

        query = q_ref[:, cols]
        scores = [
            lax.dot_general(
                query, keys, (((1,), (1,)), ((), ())), preferred_element_type=jnp.float32
            )
            * (1.0 / HEAD_DIM**0.5)
            for keys in [k_ref[:, cols]] + [rows(0, turn) for turn in range(ROUNDS)]
        ]
        peak = functools.reduce(jnp.maximum, scores)
        peak = jnp.max(peak, axis=-1, keepdims=True)
        exponents = [jnp.exp(score - peak) for score in scores]
        row_total = jnp.sum(functools.reduce(jnp.add, exponents), axis=-1, keepdims=True)
        summed = 0.0
        for exponent, values in zip(
            exponents, [v_ref[:, cols]] + [rows(1, turn) for turn in range(ROUNDS)]
        ):
            summed += jnp.dot(
                exponent.astype(jnp.bfloat16), values, preferred_element_type=jnp.float32
            )
        out_ref[:, cols] = (summed / row_total).astype(out_ref.dtype)


def attend(queries, keys, values, routed):
    in_vmem = pl.BlockSpec(memory_space=pltpu.VMEM)
    return pl.pallas_call(
        attend_kernel,
        in_specs=[in_vmem] * 4,
        out_specs=in_vmem,
        out_shape=jax.ShapeDtypeStruct(queries.shape, queries.dtype),
        compiler_params=pltpu.CompilerParams(vmem_limit_bytes=32 << 20),
        cost_estimate=pl.CostEstimate(
            flops=HINT_FLOPS, bytes_accessed=HINT_BYTES, transcendentals=0
        ),
    )(queries, keys, values, routed)


def body(queries, keys, values, plan, w_out):
    tokens, width = queries.shape
    half = lax.axis_index("zh")
    quad, member = lax.axis_index("p"), lax.axis_index("q")
    seats = lax.axis_size(PLANE)

    w_near = w_out.T
    w_far = lax.ppermute(w_near, "zh", SWAP)
    keeps_near = half == quad
    w_pair = jnp.stack(
        (jnp.where(keeps_near, w_near, w_far), jnp.where(keeps_near, w_far, w_near))
    )

    part = width // HALVES
    own = jnp.stack(
        [rows[:, h * part : (h + 1) * part] for rows in (keys, values) for h in range(HALVES)]
    )
    own = own.reshape(seats, PIECE, part)
    spread = lax.all_to_all(own, PLANE, split_axis=0, concat_axis=0, tiled=True)
    spread, w_pair = lax.optimization_barrier((spread, w_pair))

    w_pair = lax.ppermute(
        w_pair,
        ("x", "q"),
        [(x * QUAD + q, q * QUAD + x) for x in range(QUAD) for q in range(QUAD)],
    )
    far = lax.ppermute(spread, "zh", SWAP)
    w_all = lax.all_gather(w_pair, PLANE, axis=0, tiled=False)
    w_all = w_all.reshape(QUAD, seats // QUAD, 2, -1, width)

    wanted = lax.dynamic_slice_in_dim(plan, half * seats, seats, 1)
    place = (wanted // seats ^ half) * seats + wanted % seats
    chosen = jnp.concatenate((spread, far)).at[place.T].get(mode="promise_in_bounds")
    routed = lax.all_to_all(chosen, PLANE, split_axis=0, concat_axis=0, tiled=True)
    attended = attend(
        queries,
        keys,
        values,
        routed.reshape(2 * HALVES, tokens // PIECE, ROUNDS, PIECE, part),
    )

    parts = [attended] + [
        lax.ppermute(attended, "q", [(i, i ^ k) for i in range(QUAD)]) for k in range(1, QUAD)
    ]
    order = member ^ jnp.arange(QUAD, dtype=jnp.int32)
    sent = project(order, parts, w_all, 1, jnp.bfloat16)
    arrived = lax.ppermute(sent, "p", SWAP)
    kept = project(order, parts, w_all, 0, jnp.float32)
    return (kept + arrived.astype(jnp.float32)).astype(jnp.bfloat16)


def solution(mesh):
    fine = Mesh(mesh.devices.reshape(SIZES), NAMES)
    return jax.shard_map(
        body,
        mesh=fine,
        in_specs=(P(CTX, HEAD), P(CTX, HEAD), P(CTX, HEAD), P(), P(HEAD, CTX)),
        out_specs=P(CTX, HEAD),
        check_vma=False,
    )
```

```python
import functools

import jax
import jax.numpy as jnp
from jax import lax
from jax.experimental import pallas as pl
from jax.experimental.pallas import tpu as pltpu
from jax.sharding import Mesh, PartitionSpec as P

HEAD_DIM = 128
ROUNDS = 2
SIZES = (2, 4, 4, 2, 2, 4)
NAMES = ("zh", "x", "y", "c", "p", "q")
CTX = ("zh", "x", "y", "c")
HEAD = ("p", "q")
PLANE = ("x", "y", "c")
SWAP = ((0, 1), (1, 0))
QUAD = 4
HINT_FLOPS, HINT_BYTES = 120 * 10**9, 10**6
HALVES = 2
PIECE = 16


def project_kernel(order_ref, *refs, side):
    parts, (w_ref, out_ref, held, arrivals) = refs[:QUAD], refs[QUAD:]
    width = w_ref.shape[-1]
    copies = [
        pltpu.make_async_copy(w_ref.at[order_ref[k], :, side], held.at[k], arrivals.at[k])
        for k in range(QUAD)
    ]
    for copy in copies:
        copy.start()
    total = 0.0
    for k in range(QUAD):
        copies[k].wait()
        total += lax.dot_general(
            parts[k][...],
            held[k].reshape(-1, width),
            (((1,), (1,)), ((), ())),
            preferred_element_type=jnp.float32,
        )
    out_ref[...] = total.astype(out_ref.dtype)


def project(order, parts, w_all, side, dtype):
    tokens, width = parts[0].shape
    _, chunks, _, columns, _ = w_all.shape
    in_vmem = pl.BlockSpec(memory_space=pltpu.VMEM)
    return pl.pallas_call(
        functools.partial(project_kernel, side=side),
        in_specs=[pl.BlockSpec(memory_space=pltpu.SMEM)]
        + [in_vmem] * QUAD
        + [pl.BlockSpec(memory_space=pltpu.HBM)],
        out_specs=in_vmem,
        out_shape=jax.ShapeDtypeStruct((tokens, chunks * columns), dtype),
        scratch_shapes=[
            pltpu.VMEM((QUAD, chunks, columns, width), w_all.dtype),
            pltpu.SemaphoreType.DMA((QUAD,)),
        ],
        compiler_params=pltpu.CompilerParams(vmem_limit_bytes=32 << 20),
        cost_estimate=pl.CostEstimate(
            flops=2 * QUAD * tokens * width * chunks * columns,
            bytes_accessed=2 * QUAD * width * (chunks * columns + tokens),
            transcendentals=0,
        ),
    )(order, *parts, pltpu.with_memory_space_constraint(w_all, pltpu.HBM))


def attend_kernel(q_ref, k_ref, v_ref, routed_ref, out_ref):
    tokens, width = q_ref.shape
    part = width // HALVES
    for head in range(width // HEAD_DIM):
        cols = slice(head * HEAD_DIM, (head + 1) * HEAD_DIM)
        at, lane = divmod(head * HEAD_DIM, part)

        def rows(kind, turn):
            piece = routed_ref[kind * HALVES + at, :, turn, :, lane : lane + HEAD_DIM]
            return piece.reshape(tokens, HEAD_DIM)

        query = q_ref[:, cols]
        scores = [
            lax.dot_general(
                query, keys, (((1,), (1,)), ((), ())), preferred_element_type=jnp.float32
            )
            * (1.0 / HEAD_DIM**0.5)
            for keys in [k_ref[:, cols]] + [rows(0, turn) for turn in range(ROUNDS)]
        ]
        peak = functools.reduce(jnp.maximum, scores)
        peak = jnp.max(peak, axis=-1, keepdims=True)
        exponents = [jnp.exp(score - peak) for score in scores]
        row_total = jnp.sum(functools.reduce(jnp.add, exponents), axis=-1, keepdims=True)
        summed = 0.0
        for exponent, values in zip(
            exponents, [v_ref[:, cols]] + [rows(1, turn) for turn in range(ROUNDS)]
        ):
            summed += jnp.dot(
                exponent.astype(jnp.bfloat16), values, preferred_element_type=jnp.float32
            )
        out_ref[:, cols] = (summed / row_total).astype(out_ref.dtype)


def attend(queries, keys, values, routed):
    in_vmem = pl.BlockSpec(memory_space=pltpu.VMEM)
    return pl.pallas_call(
        attend_kernel,
        in_specs=[in_vmem] * 4,
        out_specs=in_vmem,
        out_shape=jax.ShapeDtypeStruct(queries.shape, queries.dtype),
        compiler_params=pltpu.CompilerParams(vmem_limit_bytes=32 << 20),
        cost_estimate=pl.CostEstimate(
            flops=HINT_FLOPS, bytes_accessed=HINT_BYTES, transcendentals=0
        ),
    )(queries, keys, values, routed)


def body(queries, keys, values, plan, w_out):
    tokens, width = queries.shape
    half = lax.axis_index("zh")
    quad, member = lax.axis_index("p"), lax.axis_index("q")
    seats = lax.axis_size(PLANE)

    w_near = w_out.T
    w_far = lax.ppermute(w_near, "zh", SWAP)
    keeps_near = half == quad
    w_pair = jnp.stack(
        (jnp.where(keeps_near, w_near, w_far), jnp.where(keeps_near, w_far, w_near))
    )

    part = width // HALVES
    own = jnp.stack(
        [rows[:, h * part : (h + 1) * part] for rows in (keys, values) for h in range(HALVES)]
    )
    own = own.reshape(seats, PIECE, part)
    spread = lax.all_to_all(own, PLANE, split_axis=0, concat_axis=0, tiled=True)
    spread, w_pair = lax.optimization_barrier((spread, w_pair))

    w_pair = lax.ppermute(
        w_pair,
        ("x", "q"),
        [(x * QUAD + q, q * QUAD + x) for x in range(QUAD) for q in range(QUAD)],
    )
    far = lax.ppermute(spread, "zh", SWAP)
    w_all = lax.all_gather(w_pair, PLANE, axis=0, tiled=False)
    w_all = w_all.reshape(QUAD, seats // QUAD, 2, -1, width)

    wanted = lax.dynamic_slice_in_dim(plan, half * seats, seats, 1)
    place = (wanted // seats ^ half) * seats + wanted % seats
    chosen = jnp.concatenate((spread, far)).at[place.T].get(mode="promise_in_bounds")
    routed = lax.all_to_all(chosen, PLANE, split_axis=0, concat_axis=0, tiled=True)
    attended = attend(
        queries,
        keys,
        values,
        routed.reshape(2 * HALVES, tokens // PIECE, ROUNDS, PIECE, part),
    )

    parts = [attended] + [
        lax.ppermute(attended, "q", [(i, i ^ k) for i in range(QUAD)]) for k in range(1, QUAD)
    ]
    order = member ^ jnp.arange(QUAD, dtype=jnp.int32)
    sent = project(order, parts, w_all, 1, jnp.bfloat16)
    arrived = lax.ppermute(sent, "p", SWAP)
    kept = project(order, parts, w_all, 0, jnp.float32)
    return (kept + arrived.astype(jnp.float32)).astype(jnp.bfloat16)


def solution(mesh):
    fine = Mesh(mesh.devices.reshape(SIZES), NAMES)
    return jax.shard_map(
        body,
        mesh=fine,
        in_specs=(P(CTX, HEAD), P(CTX, HEAD), P(CTX, HEAD), P(), P(HEAD, CTX)),
        out_specs=P(CTX, HEAD),
        check_vma=False,
    )
```

```python
import functools

import jax
import jax.numpy as jnp
from jax import lax
from jax.experimental import pallas as pl
from jax.experimental.pallas import tpu as pltpu
from jax.sharding import Mesh, PartitionSpec as P

HEAD_DIM = 128
ROUNDS = 2
SIZES = (2, 4, 4, 2, 2, 4)
NAMES = ("zh", "x", "y", "c", "p", "q")
CTX = ("zh", "x", "y", "c")
HEAD = ("p", "q")
PLANE = ("x", "y", "c")
SWAP = ((0, 1), (1, 0))
QUAD = 4
HALVES = 2
PIECE = 16


def project_kernel(place_ref, *refs):
    parts, sides, (out_ref, held, arrivals) = refs[:QUAD], refs[QUAD:-3], refs[-3:]
    width = held.shape[-1]
    core = place_ref[QUAD + 1]

    def copies(of_side):
        return [
            pltpu.make_async_copy(
                of_side[other].at[place_ref[k]],
                held.at[k, :, core ^ other],
                arrivals.at[k, other],
            )
            for k in range(QUAD)
            for other in range(2)
        ]

    for side in range(2):

        @pl.when(place_ref[QUAD] == side)
        def _(side=side):
            for copy in copies(sides[2 * side : 2 * side + 2]):
                copy.start()

    total = 0.0
    waits = copies(sides[:2])
    for k in range(QUAD):
        for wait in waits[2 * k : 2 * k + 2]:
            wait.wait()
        total += lax.dot_general(
            parts[k][...],
            held[k].reshape(-1, width),
            (((1,), (1,)), ((), ())),
            preferred_element_type=jnp.float32,
        )
    out_ref[...] = total.astype(out_ref.dtype)


def project(order, side, core, parts, near, far, dtype):
    tokens, width = parts[0].shape
    _, chunks, columns, _ = near[0].shape
    in_vmem = pl.BlockSpec(memory_space=pltpu.VMEM)
    place = jnp.concatenate((order, jnp.stack((side, core)).astype(jnp.int32)))
    return pl.pallas_call(
        project_kernel,
        in_specs=[pl.BlockSpec(memory_space=pltpu.SMEM)]
        + [in_vmem] * QUAD
        + [pl.BlockSpec(memory_space=pltpu.HBM)] * 4,
        out_specs=in_vmem,
        out_shape=jax.ShapeDtypeStruct((tokens, chunks * 2 * columns), dtype),
        scratch_shapes=[
            pltpu.VMEM((QUAD, chunks, 2, columns, width), near[0].dtype),
            pltpu.SemaphoreType.DMA((QUAD, 2)),
        ],
        compiler_params=pltpu.CompilerParams(vmem_limit_bytes=32 << 20),
        cost_estimate=pl.CostEstimate(
            flops=4 * QUAD * tokens * width * chunks * columns,
            bytes_accessed=2 * QUAD * width * (2 * chunks * columns + tokens),
            transcendentals=0,
        ),
    )(
        place,
        *parts,
        *[pltpu.with_memory_space_constraint(rows, pltpu.HBM) for rows in (*near, *far)],
    )


def attend_kernel(q_ref, k_ref, v_ref, routed_ref, out_ref):
    tokens, width = q_ref.shape
    part = width // HALVES
    for head in range(width // HEAD_DIM):
        cols = slice(head * HEAD_DIM, (head + 1) * HEAD_DIM)
        at, lane = divmod(head * HEAD_DIM, part)

        def rows(kind, turn):
            piece = routed_ref[kind * HALVES + at, :, turn, :, lane : lane + HEAD_DIM]
            return piece.reshape(tokens, HEAD_DIM)

        query = q_ref[:, cols]
        scores = [
            lax.dot_general(
                query, keys, (((1,), (1,)), ((), ())), preferred_element_type=jnp.float32
            )
            * (1.0 / HEAD_DIM**0.5)
            for keys in [k_ref[:, cols]] + [rows(0, turn) for turn in range(ROUNDS)]
        ]
        peak = functools.reduce(jnp.maximum, scores)
        peak = jnp.max(peak, axis=-1, keepdims=True)
        exponents = [jnp.exp(score - peak) for score in scores]
        row_total = jnp.sum(functools.reduce(jnp.add, exponents), axis=-1, keepdims=True)
        summed = 0.0
        for exponent, values in zip(
            exponents, [v_ref[:, cols]] + [rows(1, turn) for turn in range(ROUNDS)]
        ):
            summed += jnp.dot(
                exponent.astype(jnp.bfloat16), values, preferred_element_type=jnp.float32
            )
        out_ref[:, cols] = (summed / row_total).astype(out_ref.dtype)


def attend(queries, keys, values, routed):
    in_vmem = pl.BlockSpec(memory_space=pltpu.VMEM)
    return pl.pallas_call(
        attend_kernel,
        in_specs=[in_vmem] * 4,
        out_specs=in_vmem,
        out_shape=jax.ShapeDtypeStruct(queries.shape, queries.dtype),
        compiler_params=pltpu.CompilerParams(vmem_limit_bytes=32 << 20),
        cost_estimate=pl.CostEstimate(
            flops=4 * queries.size * (1 + ROUNDS) * queries.shape[0],
            bytes_accessed=2 * (4 * queries.size + routed.size),
            transcendentals=queries.size * (1 + ROUNDS),
        ),
    )(queries, keys, values, routed)


def body(queries, keys, values, plan, w_out):
    tokens, width = queries.shape
    half = lax.axis_index("zh")
    quad, member = lax.axis_index("p"), lax.axis_index("q")
    seats = lax.axis_size(PLANE)

    w_near, w_far = [
        lax.ppermute(
            w_out.T,
            ("zh", "x", "q"),
            [
                ((zh * QUAD + x) * QUAD + q, ((zh ^ flip) * QUAD + q) * QUAD + x)
                for zh in range(2)
                for x in range(QUAD)
                for q in range(QUAD)
            ],
        )
        for flip in range(2)
    ]

    part = width // HALVES
    own = jnp.stack(
        [rows[:, h * part : (h + 1) * part] for rows in (keys, values) for h in range(HALVES)]
    )
    own = own.reshape(seats, PIECE, part)
    spread = lax.all_to_all(own, PLANE, split_axis=0, concat_axis=0, tiled=True)
    far = lax.ppermute(spread, "zh", SWAP)

    def gather(chunk):
        to_all = jnp.broadcast_to(chunk, (QUAD * QUAD,) + chunk.shape)
        return lax.all_to_all(to_all, ("x", "y"), split_axis=0, concat_axis=0, tiled=True)

    def with_other_core(chunks):
        other = lax.ppermute(chunks, "c", SWAP)
        return [rows.reshape(QUAD, QUAD, *rows.shape[1:]) for rows in (chunks, other)]

    w_near = gather(w_near)
    far, w_near = lax.optimization_barrier((far, w_near))
    w_near = with_other_core(w_near)

    wanted = lax.dynamic_slice_in_dim(plan, half * seats, seats, 1)
    place = (wanted // seats ^ half) * seats + wanted % seats
    chosen = jnp.concatenate((spread, far)).at[place.T].get(mode="promise_in_bounds")
    routed = lax.all_to_all(chosen, PLANE, split_axis=0, concat_axis=0, tiled=True)
    routed, w_far = lax.optimization_barrier((routed, w_far))
    w_far = gather(w_far)
    attended = attend(
        queries,
        keys,
        values,
        routed.reshape(2 * HALVES, tokens // PIECE, ROUNDS, PIECE, part),
    )

    parts = [attended] + [
        lax.ppermute(attended, "q", [(i, i ^ k) for i in range(QUAD)]) for k in range(1, QUAD)
    ]
    w_far, parts = lax.optimization_barrier((w_far, parts))
    w_far = with_other_core(w_far)
    order = member ^ jnp.arange(QUAD, dtype=jnp.int32)
    core = lax.axis_index("c")
    keeps_far = (half != quad).astype(jnp.int32)
    sent = project(order, 1 - keeps_far, core, parts, w_near, w_far, jnp.bfloat16)
    arrived = lax.ppermute(sent, "p", SWAP)
    kept = project(order, keeps_far, core, parts, w_near, w_far, jnp.float32)
    return (kept + arrived.astype(jnp.float32)).astype(jnp.bfloat16)


def solution(mesh):
    fine = Mesh(mesh.devices.reshape(SIZES), NAMES)
    return jax.shard_map(
        body,
        mesh=fine,
        in_specs=(P(CTX, HEAD), P(CTX, HEAD), P(CTX, HEAD), P(), P(HEAD, CTX)),
        out_specs=P(CTX, HEAD),
        check_vma=False,
    )
```

```python
import functools

import jax
import jax.numpy as jnp
from jax import lax
from jax.experimental import pallas as pl
from jax.experimental.pallas import tpu as pltpu
from jax.sharding import Mesh, PartitionSpec as P

HEAD_DIM = 128
ROUNDS = 2
SIZES = (2, 4, 4, 2, 2, 4)
NAMES = ("zh", "x", "y", "c", "p", "q")
CTX = ("zh", "x", "y", "c")
HEAD = ("p", "q")
PLANE = ("x", "y", "c")
SWAP = ((0, 1), (1, 0))
QUAD = 4
HALVES = 2
PIECE = 16


def project_kernel(place_ref, *refs, side):
    parts, gathered, (out_ref, held, arrivals) = refs[:QUAD], refs[QUAD:-3], refs[-3:]
    width = held.shape[-1]
    core = place_ref[QUAD]
    copies = [
        [
            pltpu.make_async_copy(
                rows.at[place_ref[k], :, side],
                held.at[k, :, core ^ other],
                arrivals.at[k, other],
            )
            for other, rows in enumerate(gathered)
        ]
        for k in range(QUAD)
    ]
    for k in range(QUAD):
        for copy in copies[k]:
            copy.start()
    total = 0.0
    for k in range(QUAD):
        for copy in copies[k]:
            copy.wait()
        total += lax.dot_general(
            parts[k][...],
            held[k].reshape(-1, width),
            (((1,), (1,)), ((), ())),
            preferred_element_type=jnp.float32,
        )
    out_ref[...] = total.astype(out_ref.dtype)


def project(place, parts, gathered, side, dtype):
    tokens, width = parts[0].shape
    _, chunks, _, columns, _ = gathered[0].shape
    in_vmem = pl.BlockSpec(memory_space=pltpu.VMEM)
    return pl.pallas_call(
        functools.partial(project_kernel, side=side),
        in_specs=[pl.BlockSpec(memory_space=pltpu.SMEM)]
        + [in_vmem] * QUAD
        + [pl.BlockSpec(memory_space=pltpu.HBM)] * 2,
        out_specs=in_vmem,
        out_shape=jax.ShapeDtypeStruct((tokens, chunks * 2 * columns), dtype),
        scratch_shapes=[
            pltpu.VMEM((QUAD, chunks, 2, columns, width), gathered[0].dtype),
            pltpu.SemaphoreType.DMA((QUAD, 2)),
        ],
        compiler_params=pltpu.CompilerParams(vmem_limit_bytes=32 << 20),
        cost_estimate=pl.CostEstimate(
            flops=4 * QUAD * tokens * width * chunks * columns,
            bytes_accessed=2 * QUAD * width * (2 * chunks * columns + tokens),
            transcendentals=0,
        ),
    )(
        place,
        *parts,
        *[pltpu.with_memory_space_constraint(rows, pltpu.HBM) for rows in gathered],
    )


def attend_kernel(q_ref, k_ref, v_ref, routed_ref, out_ref):
    tokens, width = q_ref.shape
    part = width // HALVES
    for head in range(width // HEAD_DIM):
        cols = slice(head * HEAD_DIM, (head + 1) * HEAD_DIM)
        at, lane = divmod(head * HEAD_DIM, part)

        def rows(kind, turn):
            piece = routed_ref[kind * HALVES + at, :, turn, :, lane : lane + HEAD_DIM]
            return piece.reshape(tokens, HEAD_DIM)

        query = q_ref[:, cols]
        scores = [
            lax.dot_general(
                query, keys, (((1,), (1,)), ((), ())), preferred_element_type=jnp.float32
            )
            * (1.0 / HEAD_DIM**0.5)
            for keys in [k_ref[:, cols]] + [rows(0, turn) for turn in range(ROUNDS)]
        ]
        peak = functools.reduce(jnp.maximum, scores)
        peak = jnp.max(peak, axis=-1, keepdims=True)
        exponents = [jnp.exp(score - peak) for score in scores]
        row_total = jnp.sum(functools.reduce(jnp.add, exponents), axis=-1, keepdims=True)
        summed = 0.0
        for exponent, values in zip(
            exponents, [v_ref[:, cols]] + [rows(1, turn) for turn in range(ROUNDS)]
        ):
            summed += jnp.dot(
                exponent.astype(jnp.bfloat16), values, preferred_element_type=jnp.float32
            )
        out_ref[:, cols] = (summed / row_total).astype(out_ref.dtype)


def attend(queries, keys, values, routed):
    in_vmem = pl.BlockSpec(memory_space=pltpu.VMEM)
    return pl.pallas_call(
        attend_kernel,
        in_specs=[in_vmem] * 4,
        out_specs=in_vmem,
        out_shape=jax.ShapeDtypeStruct(queries.shape, queries.dtype),
        compiler_params=pltpu.CompilerParams(vmem_limit_bytes=32 << 20),
        cost_estimate=pl.CostEstimate(
            flops=4 * queries.size * (1 + ROUNDS) * queries.shape[0],
            bytes_accessed=2 * (4 * queries.size + routed.size),
            transcendentals=queries.size * (1 + ROUNDS),
        ),
    )(queries, keys, values, routed)


def body(queries, keys, values, plan, w_out):
    tokens, width = queries.shape
    half = lax.axis_index("zh")
    quad, member = lax.axis_index("p"), lax.axis_index("q")
    seats = lax.axis_size(PLANE)

    w_near, w_far = [
        lax.ppermute(
            w_out.T,
            ("zh", "x", "q"),
            [
                ((zh * QUAD + x) * QUAD + q, ((zh ^ flip) * QUAD + q) * QUAD + x)
                for zh in range(2)
                for x in range(QUAD)
                for q in range(QUAD)
            ],
        )
        for flip in range(2)
    ]

    part = width // HALVES
    own = jnp.stack(
        [rows[:, h * part : (h + 1) * part] for rows in (keys, values) for h in range(HALVES)]
    )
    own = own.reshape(seats, PIECE, part)
    spread = lax.all_to_all(own, PLANE, split_axis=0, concat_axis=0, tiled=True)
    far = lax.ppermute(spread, "zh", SWAP)

    keeps_near = half == quad
    w_pair = jnp.stack(
        (jnp.where(keeps_near, w_near, w_far), jnp.where(keeps_near, w_far, w_near))
    )
    w_all = lax.all_to_all(
        jnp.broadcast_to(w_pair, (QUAD * QUAD,) + w_pair.shape),
        ("x", "y"),
        split_axis=0,
        concat_axis=0,
        tiled=True,
    )
    far, w_all = lax.optimization_barrier((far, w_all))

    wanted = lax.dynamic_slice_in_dim(plan, half * seats, seats, 1)
    place = (wanted // seats ^ half) * seats + wanted % seats
    chosen = jnp.concatenate((spread, far)).at[place.T].get(mode="promise_in_bounds")
    routed = lax.all_to_all(chosen, PLANE, split_axis=0, concat_axis=0, tiled=True)
    gathered = [
        rows.reshape(QUAD, QUAD, *w_pair.shape) for rows in (w_all, lax.ppermute(w_all, "c", SWAP))
    ]
    attended = attend(
        queries,
        keys,
        values,
        routed.reshape(2 * HALVES, tokens // PIECE, ROUNDS, PIECE, part),
    )

    parts = [attended] + [
        lax.ppermute(attended, "q", [(i, i ^ k) for i in range(QUAD)]) for k in range(1, QUAD)
    ]
    place = jnp.append(
        member ^ jnp.arange(QUAD, dtype=jnp.int32), lax.axis_index("c").astype(jnp.int32)
    )
    sent = project(place, parts, gathered, 1, jnp.bfloat16)
    arrived = lax.ppermute(sent, "p", SWAP)
    kept = project(place, parts, gathered, 0, jnp.float32)
    return (kept + arrived.astype(jnp.float32)).astype(jnp.bfloat16)


def solution(mesh):
    fine = Mesh(mesh.devices.reshape(SIZES), NAMES)
    return jax.shard_map(
        body,
        mesh=fine,
        in_specs=(P(CTX, HEAD), P(CTX, HEAD), P(CTX, HEAD), P(), P(HEAD, CTX)),
        out_specs=P(CTX, HEAD),
        check_vma=False,
    )
```

```python
import functools

import jax
import jax.numpy as jnp
from jax import lax
from jax.experimental import pallas as pl
from jax.experimental.pallas import tpu as pltpu
from jax.sharding import Mesh, PartitionSpec as P

HEAD_DIM = 128
ROUNDS = 2
SIZES = (2, 4, 4, 2, 2, 4)
NAMES = ("zh", "x", "y", "c", "p", "q")
CTX = ("zh", "x", "y", "c")
HEAD = ("p", "q")
PLANE = ("x", "y", "c")
SWAP = ((0, 1), (1, 0))
QUAD = 4
HALVES = 2
PIECE = 16


def project_kernel(order_ref, *refs, side):
    parts, (w_ref, out_ref, held, arrivals) = refs[:QUAD], refs[QUAD:]
    width = w_ref.shape[-1]
    copies = [
        pltpu.make_async_copy(w_ref.at[order_ref[k], :, side], held.at[k], arrivals.at[k])
        for k in range(QUAD)
    ]
    for copy in copies:
        copy.start()
    total = 0.0
    for k in range(QUAD):
        copies[k].wait()
        total += lax.dot_general(
            parts[k][...],
            held[k].reshape(-1, width),
            (((1,), (1,)), ((), ())),
            preferred_element_type=jnp.float32,
        )
    out_ref[...] = total.astype(out_ref.dtype)


def project(order, parts, w_all, side, dtype):
    tokens, width = parts[0].shape
    _, chunks, _, columns, _ = w_all.shape
    in_vmem = pl.BlockSpec(memory_space=pltpu.VMEM)
    return pl.pallas_call(
        functools.partial(project_kernel, side=side),
        in_specs=[pl.BlockSpec(memory_space=pltpu.SMEM)]
        + [in_vmem] * QUAD
        + [pl.BlockSpec(memory_space=pltpu.HBM)],
        out_specs=in_vmem,
        out_shape=jax.ShapeDtypeStruct((tokens, chunks * columns), dtype),
        scratch_shapes=[
            pltpu.VMEM((QUAD, chunks, columns, width), w_all.dtype),
            pltpu.SemaphoreType.DMA((QUAD,)),
        ],
        compiler_params=pltpu.CompilerParams(vmem_limit_bytes=32 << 20),
        cost_estimate=pl.CostEstimate(
            flops=2 * QUAD * tokens * width * chunks * columns,
            bytes_accessed=2 * QUAD * width * (chunks * columns + tokens),
            transcendentals=0,
        ),
    )(order, *parts, pltpu.with_memory_space_constraint(w_all, pltpu.HBM))


def attend_kernel(q_ref, k_ref, v_ref, routed_ref, out_ref):
    tokens, width = q_ref.shape
    part = width // HALVES
    for head in range(width // HEAD_DIM):
        cols = slice(head * HEAD_DIM, (head + 1) * HEAD_DIM)
        at, lane = divmod(head * HEAD_DIM, part)

        def rows(kind, turn):
            piece = routed_ref[kind * HALVES + at, :, turn, :, lane : lane + HEAD_DIM]
            return piece.reshape(tokens, HEAD_DIM)

        query = q_ref[:, cols]
        scores = [
            lax.dot_general(
                query, keys, (((1,), (1,)), ((), ())), preferred_element_type=jnp.float32
            )
            * (1.0 / HEAD_DIM**0.5)
            for keys in [k_ref[:, cols]] + [rows(0, turn) for turn in range(ROUNDS)]
        ]
        peak = functools.reduce(jnp.maximum, scores)
        peak = jnp.max(peak, axis=-1, keepdims=True)
        exponents = [jnp.exp(score - peak) for score in scores]
        row_total = jnp.sum(functools.reduce(jnp.add, exponents), axis=-1, keepdims=True)
        summed = 0.0
        for exponent, values in zip(
            exponents, [v_ref[:, cols]] + [rows(1, turn) for turn in range(ROUNDS)]
        ):
            summed += jnp.dot(
                exponent.astype(jnp.bfloat16), values, preferred_element_type=jnp.float32
            )
        out_ref[:, cols] = (summed / row_total).astype(out_ref.dtype)


def attend(queries, keys, values, routed):
    in_vmem = pl.BlockSpec(memory_space=pltpu.VMEM)
    return pl.pallas_call(
        attend_kernel,
        in_specs=[in_vmem] * 4,
        out_specs=in_vmem,
        out_shape=jax.ShapeDtypeStruct(queries.shape, queries.dtype),
        compiler_params=pltpu.CompilerParams(vmem_limit_bytes=32 << 20),
        cost_estimate=pl.CostEstimate(
            flops=4 * queries.size * (1 + ROUNDS) * queries.shape[0],
            bytes_accessed=2 * (4 * queries.size + routed.size),
            transcendentals=queries.size * (1 + ROUNDS),
        ),
    )(queries, keys, values, routed)


def body(queries, keys, values, plan, w_out):
    tokens, width = queries.shape
    half = lax.axis_index("zh")
    quad, member = lax.axis_index("p"), lax.axis_index("q")
    seats = lax.axis_size(PLANE)

    w_near, w_far = [
        lax.ppermute(
            w_out.T,
            ("zh", "x", "q"),
            [
                ((zh * QUAD + x) * QUAD + q, ((zh ^ flip) * QUAD + q) * QUAD + x)
                for zh in range(2)
                for x in range(QUAD)
                for q in range(QUAD)
            ],
        )
        for flip in range(2)
    ]
    keeps_near = half == quad
    w_pair = jnp.stack(
        (jnp.where(keeps_near, w_near, w_far), jnp.where(keeps_near, w_far, w_near))
    )

    part = width // HALVES
    own = jnp.stack(
        [rows[:, h * part : (h + 1) * part] for rows in (keys, values) for h in range(HALVES)]
    )
    own = own.reshape(seats, PIECE, part)
    spread = lax.all_to_all(own, PLANE, split_axis=0, concat_axis=0, tiled=True)

    token = jnp.zeros((seats, 8, 128), jnp.bfloat16)
    token, w_pair, spread = lax.optimization_barrier((token, w_pair, spread))
    token = lax.all_to_all(token, PLANE, split_axis=0, concat_axis=0, tiled=True)
    spread = spread + token[0, 0, 0]
    far = lax.ppermute(spread, "zh", SWAP)
    w_all = lax.all_gather(w_pair, PLANE, axis=0, tiled=False)
    w_all = w_all.reshape(QUAD, seats // QUAD, 2, -1, width)

    wanted = lax.dynamic_slice_in_dim(plan, half * seats, seats, 1)
    place = (wanted // seats ^ half) * seats + wanted % seats
    chosen = jnp.concatenate((spread, far)).at[place.T].get(mode="promise_in_bounds")
    routed = lax.all_to_all(chosen, PLANE, split_axis=0, concat_axis=0, tiled=True)
    attended = attend(
        queries,
        keys,
        values,
        routed.reshape(2 * HALVES, tokens // PIECE, ROUNDS, PIECE, part),
    )

    parts = [attended] + [
        lax.ppermute(attended, "q", [(i, i ^ k) for i in range(QUAD)]) for k in range(1, QUAD)
    ]
    order = member ^ jnp.arange(QUAD, dtype=jnp.int32)
    sent = project(order, parts, w_all, 1, jnp.bfloat16)
    arrived = lax.ppermute(sent, "p", SWAP)
    kept = project(order, parts, w_all, 0, jnp.float32)
    return (kept + arrived.astype(jnp.float32)).astype(jnp.bfloat16)


def solution(mesh):
    fine = Mesh(mesh.devices.reshape(SIZES), NAMES)
    return jax.shard_map(
        body,
        mesh=fine,
        in_specs=(P(CTX, HEAD), P(CTX, HEAD), P(CTX, HEAD), P(), P(HEAD, CTX)),
        out_specs=P(CTX, HEAD),
        check_vma=False,
    )
```

```python
import functools

import jax
import jax.numpy as jnp
from jax import lax
from jax.experimental import pallas as pl
from jax.experimental.pallas import tpu as pltpu
from jax.sharding import Mesh, PartitionSpec as P

HEAD_DIM = 128
ROUNDS = 2
SIZES = (2, 4, 4, 2, 2, 4)
NAMES = ("zh", "x", "y", "c", "p", "q")
CTX = ("zh", "x", "y", "c")
HEAD = ("p", "q")
PLANE = ("x", "y", "c")
SWAP = ((0, 1), (1, 0))
QUAD = 4
HINT_FLOPS, HINT_BYTES = 183 * 10**9, 10**6
HALVES = 2
PIECE = 16


def project_kernel(order_ref, *refs, side):
    parts, (w_ref, out_ref, held, arrivals) = refs[:QUAD], refs[QUAD:]
    width = w_ref.shape[-1]
    copies = [
        pltpu.make_async_copy(w_ref.at[order_ref[k], :, side], held.at[k], arrivals.at[k])
        for k in range(QUAD)
    ]
    for copy in copies:
        copy.start()
    total = 0.0
    for k in range(QUAD):
        copies[k].wait()
        total += lax.dot_general(
            parts[k][...],
            held[k].reshape(-1, width),
            (((1,), (1,)), ((), ())),
            preferred_element_type=jnp.float32,
        )
    out_ref[...] = total.astype(out_ref.dtype)


def project(order, parts, w_all, side, dtype):
    tokens, width = parts[0].shape
    _, chunks, _, columns, _ = w_all.shape
    in_vmem = pl.BlockSpec(memory_space=pltpu.VMEM)
    return pl.pallas_call(
        functools.partial(project_kernel, side=side),
        in_specs=[pl.BlockSpec(memory_space=pltpu.SMEM)]
        + [in_vmem] * QUAD
        + [pl.BlockSpec(memory_space=pltpu.HBM)],
        out_specs=in_vmem,
        out_shape=jax.ShapeDtypeStruct((tokens, chunks * columns), dtype),
        scratch_shapes=[
            pltpu.VMEM((QUAD, chunks, columns, width), w_all.dtype),
            pltpu.SemaphoreType.DMA((QUAD,)),
        ],
        compiler_params=pltpu.CompilerParams(vmem_limit_bytes=32 << 20),
        cost_estimate=pl.CostEstimate(
            flops=2 * QUAD * tokens * width * chunks * columns,
            bytes_accessed=2 * QUAD * width * (chunks * columns + tokens),
            transcendentals=0,
        ),
    )(order, *parts, pltpu.with_memory_space_constraint(w_all, pltpu.HBM))


def attend_kernel(q_ref, k_ref, v_ref, routed_ref, out_ref):
    tokens, width = q_ref.shape
    part = width // HALVES
    for head in range(width // HEAD_DIM):
        cols = slice(head * HEAD_DIM, (head + 1) * HEAD_DIM)
        at, lane = divmod(head * HEAD_DIM, part)

        def rows(kind, turn):
            piece = routed_ref[kind * HALVES + at, :, turn, :, lane : lane + HEAD_DIM]
            return piece.reshape(tokens, HEAD_DIM)

        query = q_ref[:, cols]
        scores = [
            lax.dot_general(
                query, keys, (((1,), (1,)), ((), ())), preferred_element_type=jnp.float32
            )
            * (1.0 / HEAD_DIM**0.5)
            for keys in [k_ref[:, cols]] + [rows(0, turn) for turn in range(ROUNDS)]
        ]
        peak = functools.reduce(jnp.maximum, scores)
        peak = jnp.max(peak, axis=-1, keepdims=True)
        exponents = [jnp.exp(score - peak) for score in scores]
        row_total = jnp.sum(functools.reduce(jnp.add, exponents), axis=-1, keepdims=True)
        summed = 0.0
        for exponent, values in zip(
            exponents, [v_ref[:, cols]] + [rows(1, turn) for turn in range(ROUNDS)]
        ):
            summed += jnp.dot(
                exponent.astype(jnp.bfloat16), values, preferred_element_type=jnp.float32
            )
        out_ref[:, cols] = (summed / row_total).astype(out_ref.dtype)


def attend(queries, keys, values, routed):
    in_vmem = pl.BlockSpec(memory_space=pltpu.VMEM)
    return pl.pallas_call(
        attend_kernel,
        in_specs=[in_vmem] * 4,
        out_specs=in_vmem,
        out_shape=jax.ShapeDtypeStruct(queries.shape, queries.dtype),
        compiler_params=pltpu.CompilerParams(vmem_limit_bytes=32 << 20),
        cost_estimate=pl.CostEstimate(
            flops=HINT_FLOPS, bytes_accessed=HINT_BYTES, transcendentals=0
        ),
    )(queries, keys, values, routed)


def body(queries, keys, values, plan, w_out):
    tokens, width = queries.shape
    half = lax.axis_index("zh")
    quad, member = lax.axis_index("p"), lax.axis_index("q")
    seats = lax.axis_size(PLANE)

    w_near = lax.ppermute(
        w_out.T,
        ("x", "q"),
        [(x * QUAD + q, q * QUAD + x) for x in range(QUAD) for q in range(QUAD)],
    )

    part = width // HALVES
    own = jnp.stack(
        [rows[:, h * part : (h + 1) * part] for rows in (keys, values) for h in range(HALVES)]
    )
    own = own.reshape(seats, PIECE, part)
    spread = lax.all_to_all(own, PLANE, split_axis=0, concat_axis=0, tiled=True)
    spread, w_near = lax.optimization_barrier((spread, w_near))

    w_far = lax.ppermute(w_near, "zh", SWAP)
    keeps_near = half == quad
    w_pair = jnp.stack(
        (jnp.where(keeps_near, w_near, w_far), jnp.where(keeps_near, w_far, w_near))
    )
    spread = jnp.split(spread, 2)
    far = [lax.ppermute(spread[0], "zh", SWAP)]
    spread[1], w_pair = lax.optimization_barrier((spread[1], w_pair))
    far.append(lax.ppermute(spread[1], "zh", SWAP))
    w_all = lax.all_gather(w_pair, PLANE, axis=0, tiled=False)
    w_all = w_all.reshape(QUAD, seats // QUAD, 2, -1, width)

    wanted = lax.dynamic_slice_in_dim(plan, half * seats, seats, 1)
    place = (wanted // seats ^ half) * seats + wanted % seats
    chosen = jnp.concatenate((*spread, *far)).at[place.T].get(mode="promise_in_bounds")
    routed = lax.all_to_all(chosen, PLANE, split_axis=0, concat_axis=0, tiled=True)
    attended = attend(
        queries,
        keys,
        values,
        routed.reshape(2 * HALVES, tokens // PIECE, ROUNDS, PIECE, part),
    )

    parts = [attended] + [
        lax.ppermute(attended, "q", [(i, i ^ k) for i in range(QUAD)]) for k in range(1, QUAD)
    ]
    order = member ^ jnp.arange(QUAD, dtype=jnp.int32)
    sent = project(order, parts, w_all, 1, jnp.bfloat16)
    arrived = lax.ppermute(sent, "p", SWAP)
    kept = project(order, parts, w_all, 0, jnp.float32)
    return (kept + arrived.astype(jnp.float32)).astype(jnp.bfloat16)


def solution(mesh):
    fine = Mesh(mesh.devices.reshape(SIZES), NAMES)
    return jax.shard_map(
        body,
        mesh=fine,
        in_specs=(P(CTX, HEAD), P(CTX, HEAD), P(CTX, HEAD), P(), P(HEAD, CTX)),
        out_specs=P(CTX, HEAD),
        check_vma=False,
    )
```

```python
import functools

import jax
import jax.numpy as jnp
from jax import lax
from jax.experimental import pallas as pl
from jax.experimental.pallas import tpu as pltpu
from jax.sharding import Mesh, PartitionSpec as P

HEAD_DIM = 128
ROUNDS = 2
SIZES = (2, 4, 4, 2, 2, 4)
NAMES = ("zh", "x", "y", "c", "p", "q")
CTX = ("zh", "x", "y", "c")
HEAD = ("p", "q")
PLANE = ("x", "y", "c")
SWAP = ((0, 1), (1, 0))
QUAD = 4
HALVES = 2
PIECE = 16


def project_kernel(order_ref, *refs, side):
    parts, (w_ref, out_ref, held, arrivals) = refs[:QUAD], refs[QUAD:]
    width = w_ref.shape[-1]
    copies = [
        pltpu.make_async_copy(w_ref.at[order_ref[k], :, side], held.at[k], arrivals.at[k])
        for k in range(QUAD)
    ]
    for copy in copies:
        copy.start()
    total = 0.0
    for k in range(QUAD):
        copies[k].wait()
        total += lax.dot_general(
            parts[k][...],
            held[k].reshape(-1, width),
            (((1,), (1,)), ((), ())),
            preferred_element_type=jnp.float32,
        )
    out_ref[...] = total.astype(out_ref.dtype)


def project(order, parts, w_all, side, dtype):
    tokens, width = parts[0].shape
    _, chunks, _, columns, _ = w_all.shape
    in_vmem = pl.BlockSpec(memory_space=pltpu.VMEM)
    return pl.pallas_call(
        functools.partial(project_kernel, side=side),
        in_specs=[pl.BlockSpec(memory_space=pltpu.SMEM)]
        + [in_vmem] * QUAD
        + [pl.BlockSpec(memory_space=pltpu.HBM)],
        out_specs=in_vmem,
        out_shape=jax.ShapeDtypeStruct((tokens, chunks * columns), dtype),
        scratch_shapes=[
            pltpu.VMEM((QUAD, chunks, columns, width), w_all.dtype),
            pltpu.SemaphoreType.DMA((QUAD,)),
        ],
        compiler_params=pltpu.CompilerParams(vmem_limit_bytes=32 << 20),
        cost_estimate=pl.CostEstimate(
            flops=2 * QUAD * tokens * width * chunks * columns,
            bytes_accessed=2 * QUAD * width * (chunks * columns + tokens),
            transcendentals=0,
        ),
    )(order, *parts, pltpu.with_memory_space_constraint(w_all, pltpu.HBM))


def attend_kernel(q_ref, k_ref, v_ref, routed_ref, out_ref):
    tokens, width = q_ref.shape
    part = width // HALVES
    for head in range(width // HEAD_DIM):
        cols = slice(head * HEAD_DIM, (head + 1) * HEAD_DIM)
        at, lane = divmod(head * HEAD_DIM, part)

        def rows(kind, turn):
            piece = routed_ref[kind * HALVES + at, :, turn, :, lane : lane + HEAD_DIM]
            return piece.reshape(tokens, HEAD_DIM)

        query = q_ref[:, cols]
        scores = [
            lax.dot_general(
                query, keys, (((1,), (1,)), ((), ())), preferred_element_type=jnp.float32
            )
            * (1.0 / HEAD_DIM**0.5)
            for keys in [k_ref[:, cols]] + [rows(0, turn) for turn in range(ROUNDS)]
        ]
        peak = functools.reduce(jnp.maximum, scores)
        peak = jnp.max(peak, axis=-1, keepdims=True)
        exponents = [jnp.exp(score - peak) for score in scores]
        row_total = jnp.sum(functools.reduce(jnp.add, exponents), axis=-1, keepdims=True)
        summed = 0.0
        for exponent, values in zip(
            exponents, [v_ref[:, cols]] + [rows(1, turn) for turn in range(ROUNDS)]
        ):
            summed += jnp.dot(
                exponent.astype(jnp.bfloat16), values, preferred_element_type=jnp.float32
            )
        out_ref[:, cols] = (summed / row_total).astype(out_ref.dtype)


def attend(queries, keys, values, routed):
    in_vmem = pl.BlockSpec(memory_space=pltpu.VMEM)
    return pl.pallas_call(
        attend_kernel,
        in_specs=[in_vmem] * 4,
        out_specs=in_vmem,
        out_shape=jax.ShapeDtypeStruct(queries.shape, queries.dtype),
        compiler_params=pltpu.CompilerParams(vmem_limit_bytes=32 << 20),
        cost_estimate=pl.CostEstimate(
            flops=4 * queries.size * (1 + ROUNDS) * queries.shape[0],
            bytes_accessed=2 * (4 * queries.size + routed.size),
            transcendentals=queries.size * (1 + ROUNDS),
        ),
    )(queries, keys, values, routed)


def body(queries, keys, values, plan, w_out):
    tokens, width = queries.shape
    half = lax.axis_index("zh")
    quad, member = lax.axis_index("p"), lax.axis_index("q")
    seats = lax.axis_size(PLANE)

    w_near = lax.ppermute(
        w_out.T,
        ("x", "q"),
        [(x * QUAD + q, q * QUAD + x) for x in range(QUAD) for q in range(QUAD)],
    )

    part = width // HALVES
    own = jnp.stack(
        [rows[:, h * part : (h + 1) * part] for rows in (keys, values) for h in range(HALVES)]
    )
    own = own.reshape(seats, PIECE, part)
    spread = lax.all_to_all(own, PLANE, split_axis=0, concat_axis=0, tiled=True)
    spread, w_near = lax.optimization_barrier((spread, w_near))

    w_far = lax.ppermute(w_near, "zh", SWAP)
    far = lax.ppermute(spread, "zh", SWAP)
    keeps_near = half == quad
    w_pair = jnp.stack(
        (jnp.where(keeps_near, w_near, w_far), jnp.where(keeps_near, w_far, w_near))
    )
    w_all = lax.all_gather(w_pair, PLANE, axis=0, tiled=False)
    w_all = w_all.reshape(QUAD, seats // QUAD, 2, -1, width)

    wanted = lax.dynamic_slice_in_dim(plan, half * seats, seats, 1)
    place = (wanted // seats ^ half) * seats + wanted % seats
    chosen = jnp.concatenate((spread, far)).at[place.T].get(mode="promise_in_bounds")
    routed = lax.all_to_all(chosen, PLANE, split_axis=0, concat_axis=0, tiled=True)
    attended = attend(
        queries,
        keys,
        values,
        routed.reshape(2 * HALVES, tokens // PIECE, ROUNDS, PIECE, part),
    )

    parts = [attended] + [
        lax.ppermute(attended, "q", [(i, i ^ k) for i in range(QUAD)]) for k in range(1, QUAD)
    ]
    order = member ^ jnp.arange(QUAD, dtype=jnp.int32)
    sent = project(order, parts, w_all, 1, jnp.bfloat16)
    arrived = lax.ppermute(sent, "p", SWAP)
    kept = project(order, parts, w_all, 0, jnp.float32)
    return (kept + arrived.astype(jnp.float32)).astype(jnp.bfloat16)


def solution(mesh):
    fine = Mesh(mesh.devices.reshape(SIZES), NAMES)
    return jax.shard_map(
        body,
        mesh=fine,
        in_specs=(P(CTX, HEAD), P(CTX, HEAD), P(CTX, HEAD), P(), P(HEAD, CTX)),
        out_specs=P(CTX, HEAD),
        check_vma=False,
    )
```

```python
import functools

import jax
import jax.numpy as jnp
from jax import lax
from jax.experimental import pallas as pl
from jax.experimental.pallas import tpu as pltpu
from jax.sharding import Mesh, PartitionSpec as P

HEAD_DIM = 128
ROUNDS = 2
SIZES = (2, 4, 4, 2, 2, 4)
NAMES = ("zh", "x", "y", "c", "p", "q")
CTX = ("zh", "x", "y", "c")
HEAD = ("p", "q")
PLANE = ("x", "y", "c")
SWAP = ((0, 1), (1, 0))
QUAD = 4
HALVES = 2
PIECE = 16


def project_kernel(place_ref, *refs):
    parts, sides, (out_ref, held, arrivals) = refs[:QUAD], refs[QUAD:-3], refs[-3:]
    width = held.shape[-1]
    core = place_ref[QUAD + 1]

    def copies(of_side):
        return [
            pltpu.make_async_copy(
                of_side[other].at[place_ref[k]],
                held.at[k, :, core ^ other],
                arrivals.at[k, other],
            )
            for k in range(QUAD)
            for other in range(2)
        ]

    for side in range(2):

        @pl.when(place_ref[QUAD] == side)
        def _(side=side):
            for copy in copies(sides[2 * side : 2 * side + 2]):
                copy.start()

    total = 0.0
    waits = copies(sides[:2])
    for k in range(QUAD):
        for wait in waits[2 * k : 2 * k + 2]:
            wait.wait()
        total += lax.dot_general(
            parts[k][...],
            held[k].reshape(-1, width),
            (((1,), (1,)), ((), ())),
            preferred_element_type=jnp.float32,
        )
    out_ref[...] = total.astype(out_ref.dtype)


def project(order, side, core, parts, near, far, dtype):
    tokens, width = parts[0].shape
    _, chunks, columns, _ = near[0].shape
    in_vmem = pl.BlockSpec(memory_space=pltpu.VMEM)
    place = jnp.concatenate((order, jnp.stack((side, core)).astype(jnp.int32)))
    return pl.pallas_call(
        project_kernel,
        in_specs=[pl.BlockSpec(memory_space=pltpu.SMEM)]
        + [in_vmem] * QUAD
        + [pl.BlockSpec(memory_space=pltpu.HBM)] * 4,
        out_specs=in_vmem,
        out_shape=jax.ShapeDtypeStruct((tokens, chunks * 2 * columns), dtype),
        scratch_shapes=[
            pltpu.VMEM((QUAD, chunks, 2, columns, width), near[0].dtype),
            pltpu.SemaphoreType.DMA((QUAD, 2)),
        ],
        compiler_params=pltpu.CompilerParams(vmem_limit_bytes=32 << 20),
        cost_estimate=pl.CostEstimate(
            flops=4 * QUAD * tokens * width * chunks * columns,
            bytes_accessed=2 * QUAD * width * (2 * chunks * columns + tokens),
            transcendentals=0,
        ),
    )(
        place,
        *parts,
        *[pltpu.with_memory_space_constraint(rows, pltpu.HBM) for rows in (*near, *far)],
    )


def attend_kernel(q_ref, k_ref, v_ref, routed_ref, out_ref):
    tokens, width = q_ref.shape
    part = width // HALVES
    for head in range(width // HEAD_DIM):
        cols = slice(head * HEAD_DIM, (head + 1) * HEAD_DIM)
        at, lane = divmod(head * HEAD_DIM, part)

        def rows(kind, turn):
            piece = routed_ref[kind * HALVES + at, :, turn, :, lane : lane + HEAD_DIM]
            return piece.reshape(tokens, HEAD_DIM)

        query = q_ref[:, cols]
        scores = [
            lax.dot_general(
                query, keys, (((1,), (1,)), ((), ())), preferred_element_type=jnp.float32
            )
            * (1.0 / HEAD_DIM**0.5)
            for keys in [k_ref[:, cols]] + [rows(0, turn) for turn in range(ROUNDS)]
        ]
        peak = functools.reduce(jnp.maximum, scores)
        peak = jnp.max(peak, axis=-1, keepdims=True)
        exponents = [jnp.exp(score - peak) for score in scores]
        row_total = jnp.sum(functools.reduce(jnp.add, exponents), axis=-1, keepdims=True)
        summed = 0.0
        for exponent, values in zip(
            exponents, [v_ref[:, cols]] + [rows(1, turn) for turn in range(ROUNDS)]
        ):
            summed += jnp.dot(
                exponent.astype(jnp.bfloat16), values, preferred_element_type=jnp.float32
            )
        out_ref[:, cols] = (summed / row_total).astype(out_ref.dtype)


def attend(queries, keys, values, routed):
    in_vmem = pl.BlockSpec(memory_space=pltpu.VMEM)
    return pl.pallas_call(
        attend_kernel,
        in_specs=[in_vmem] * 4,
        out_specs=in_vmem,
        out_shape=jax.ShapeDtypeStruct(queries.shape, queries.dtype),
        compiler_params=pltpu.CompilerParams(vmem_limit_bytes=32 << 20),
        cost_estimate=pl.CostEstimate(
            flops=4 * queries.size * (1 + ROUNDS) * queries.shape[0],
            bytes_accessed=2 * (4 * queries.size + routed.size),
            transcendentals=queries.size * (1 + ROUNDS),
        ),
    )(queries, keys, values, routed)


def body(queries, keys, values, plan, w_out):
    tokens, width = queries.shape
    half = lax.axis_index("zh")
    quad, member = lax.axis_index("p"), lax.axis_index("q")
    seats = lax.axis_size(PLANE)

    w_near = lax.ppermute(
        w_out.T,
        ("x", "q"),
        [(x * QUAD + q, q * QUAD + x) for x in range(QUAD) for q in range(QUAD)],
    )

    part = width // HALVES
    own = jnp.stack(
        [rows[:, h * part : (h + 1) * part] for rows in (keys, values) for h in range(HALVES)]
    )
    own = own.reshape(seats, PIECE, part)
    spread = lax.all_to_all(own, PLANE, split_axis=0, concat_axis=0, tiled=True)
    far = lax.ppermute(spread, "zh", SWAP)

    w_far = lax.ppermute(w_near, "zh", SWAP)

    def gather(chunk):
        to_all = jnp.broadcast_to(chunk, (QUAD * QUAD,) + chunk.shape)
        return lax.all_to_all(to_all, ("x", "y"), split_axis=0, concat_axis=0, tiled=True)

    def with_other_core(chunks):
        other = lax.ppermute(chunks, "c", SWAP)
        return [rows.reshape(QUAD, QUAD, *rows.shape[1:]) for rows in (chunks, other)]

    w_near = gather(w_near)
    far, w_near, w_far = lax.optimization_barrier((far, w_near, w_far))
    w_near = with_other_core(w_near)

    wanted = lax.dynamic_slice_in_dim(plan, half * seats, seats, 1)
    place = (wanted // seats ^ half) * seats + wanted % seats
    chosen = jnp.concatenate((spread, far)).at[place.T].get(mode="promise_in_bounds")
    routed = lax.all_to_all(chosen, PLANE, split_axis=0, concat_axis=0, tiled=True)
    routed, w_far = lax.optimization_barrier((routed, w_far))
    w_far = gather(w_far)
    attended = attend(
        queries,
        keys,
        values,
        routed.reshape(2 * HALVES, tokens // PIECE, ROUNDS, PIECE, part),
    )

    parts = [attended] + [
        lax.ppermute(attended, "q", [(i, i ^ k) for i in range(QUAD)]) for k in range(1, QUAD)
    ]
    w_far, parts = lax.optimization_barrier((w_far, parts))
    w_far = with_other_core(w_far)
    order = member ^ jnp.arange(QUAD, dtype=jnp.int32)
    core = lax.axis_index("c")
    keeps_far = (half != quad).astype(jnp.int32)
    sent = project(order, 1 - keeps_far, core, parts, w_near, w_far, jnp.bfloat16)
    arrived = lax.ppermute(sent, "p", SWAP)
    kept = project(order, keeps_far, core, parts, w_near, w_far, jnp.float32)
    return (kept + arrived.astype(jnp.float32)).astype(jnp.bfloat16)


def solution(mesh):
    fine = Mesh(mesh.devices.reshape(SIZES), NAMES)
    return jax.shard_map(
        body,
        mesh=fine,
        in_specs=(P(CTX, HEAD), P(CTX, HEAD), P(CTX, HEAD), P(), P(HEAD, CTX)),
        out_specs=P(CTX, HEAD),
        check_vma=False,
    )
```

```python
import functools

import jax
import jax.numpy as jnp
from jax import lax
from jax.experimental import pallas as pl
from jax.experimental.pallas import tpu as pltpu
from jax.sharding import Mesh, PartitionSpec as P

HEAD_DIM = 128
ROUNDS = 2
SIZES = (2, 4, 4, 2, 2, 4)
NAMES = ("zh", "x", "y", "c", "p", "q")
CTX = ("zh", "x", "y", "c")
HEAD = ("p", "q")
PLANE = ("x", "y", "c")
SWAP = ((0, 1), (1, 0))
QUAD = 4
HALVES = 2
PIECE = 16


def project_kernel(order_ref, *refs, side):
    parts, (w_ref, out_ref, held, arrivals) = refs[:QUAD], refs[QUAD:]
    width = w_ref.shape[-1]
    copies = [
        pltpu.make_async_copy(w_ref.at[order_ref[k], :, side], held.at[k], arrivals.at[k])
        for k in range(QUAD)
    ]
    for copy in copies:
        copy.start()
    total = 0.0
    for k in range(QUAD):
        copies[k].wait()
        total += lax.dot_general(
            held[k].reshape(-1, width),
            parts[k][...],
            (((1,), (1,)), ((), ())),
            preferred_element_type=jnp.float32,
        )
    out_ref[...] = total.T.astype(out_ref.dtype)


def project(order, parts, w_all, side, dtype):
    tokens, width = parts[0].shape
    _, chunks, _, columns, _ = w_all.shape
    in_vmem = pl.BlockSpec(memory_space=pltpu.VMEM)
    return pl.pallas_call(
        functools.partial(project_kernel, side=side),
        in_specs=[pl.BlockSpec(memory_space=pltpu.SMEM)]
        + [in_vmem] * QUAD
        + [pl.BlockSpec(memory_space=pltpu.HBM)],
        out_specs=in_vmem,
        out_shape=jax.ShapeDtypeStruct((tokens, chunks * columns), dtype),
        scratch_shapes=[
            pltpu.VMEM((QUAD, chunks, columns, width), w_all.dtype),
            pltpu.SemaphoreType.DMA((QUAD,)),
        ],
        compiler_params=pltpu.CompilerParams(vmem_limit_bytes=32 << 20),
        cost_estimate=pl.CostEstimate(
            flops=2 * QUAD * tokens * width * chunks * columns,
            bytes_accessed=2 * QUAD * width * (chunks * columns + tokens),
            transcendentals=0,
        ),
    )(order, *parts, pltpu.with_memory_space_constraint(w_all, pltpu.HBM))


def attend_kernel(own_ref, routed_ref, out_ref):
    _, tokens, width = own_ref.shape
    part = width // HALVES
    for head in range(width // HEAD_DIM):
        cols = slice(head * HEAD_DIM, (head + 1) * HEAD_DIM)
        at, lane = divmod(head * HEAD_DIM, part)

        def rows(kind, turn):
            piece = routed_ref[kind * HALVES + at, :, turn, :, lane : lane + HEAD_DIM]
            return piece.reshape(tokens, HEAD_DIM)

        query = own_ref[0, :, cols]
        scores = [
            lax.dot_general(
                query, keys, (((1,), (1,)), ((), ())), preferred_element_type=jnp.float32
            )
            * (1.0 / HEAD_DIM**0.5)
            for keys in [own_ref[1, :, cols]] + [rows(0, turn) for turn in range(ROUNDS)]
        ]
        peak = functools.reduce(jnp.maximum, scores)
        peak = jnp.max(peak, axis=-1, keepdims=True)
        exponents = [jnp.exp(score - peak) for score in scores]
        row_total = jnp.sum(functools.reduce(jnp.add, exponents), axis=-1, keepdims=True)
        summed = 0.0
        for exponent, values in zip(
            exponents, [own_ref[2, :, cols]] + [rows(1, turn) for turn in range(ROUNDS)]
        ):
            summed += jnp.dot(
                exponent.astype(jnp.bfloat16), values, preferred_element_type=jnp.float32
            )
        out_ref[:, cols] = (summed / row_total).astype(out_ref.dtype)


def attend(own, routed):
    _, tokens, width = own.shape
    in_vmem = pl.BlockSpec(memory_space=pltpu.VMEM)
    return pl.pallas_call(
        attend_kernel,
        in_specs=[in_vmem] * 2,
        out_specs=in_vmem,
        out_shape=jax.ShapeDtypeStruct((tokens, width), own.dtype),
        compiler_params=pltpu.CompilerParams(vmem_limit_bytes=32 << 20),
        cost_estimate=pl.CostEstimate(
            flops=4 * tokens * width * (1 + ROUNDS) * tokens,
            bytes_accessed=2 * (own.size + routed.size + tokens * width),
            transcendentals=tokens * width * (1 + ROUNDS),
        ),
    )(own, routed)


def body(queries, keys, values, plan, w_out):
    tokens, width = queries.shape
    half = lax.axis_index("zh")
    quad, member = lax.axis_index("p"), lax.axis_index("q")
    seats = lax.axis_size(PLANE)

    w_near = lax.ppermute(
        w_out.T,
        ("x", "q"),
        [(x * QUAD + q, q * QUAD + x) for x in range(QUAD) for q in range(QUAD)],
    )

    part = width // HALVES
    own = jnp.stack(
        [rows[:, h * part : (h + 1) * part] for rows in (keys, values) for h in range(HALVES)]
    )
    own = own.reshape(seats, PIECE, part)
    spread = lax.all_to_all(own, PLANE, split_axis=0, concat_axis=0, tiled=True)
    spread, w_near = lax.optimization_barrier((spread, w_near))

    w_far = lax.ppermute(w_near, "zh", SWAP)
    far = lax.ppermute(spread, "zh", SWAP)
    keeps_near = half == quad
    w_pair = jnp.stack(
        (jnp.where(keeps_near, w_near, w_far), jnp.where(keeps_near, w_far, w_near))
    )
    w_all = lax.all_gather(w_pair, PLANE, axis=0, tiled=False)
    w_all = w_all.reshape(QUAD, seats // QUAD, 2, -1, width)

    block = jnp.stack((queries, keys, values))
    far, block = lax.optimization_barrier((far, block))

    wanted = lax.dynamic_slice_in_dim(plan, half * seats, seats, 1)
    place = (wanted // seats ^ half) * seats + wanted % seats
    chosen = jnp.concatenate((spread, far)).at[place.T].get(mode="promise_in_bounds")
    routed = lax.all_to_all(chosen, PLANE, split_axis=0, concat_axis=0, tiled=True)
    attended = attend(
        block, routed.reshape(2 * HALVES, tokens // PIECE, ROUNDS, PIECE, part)
    )

    parts = [attended] + [
        lax.ppermute(attended, "q", [(i, i ^ k) for i in range(QUAD)]) for k in range(1, QUAD)
    ]
    order = member ^ jnp.arange(QUAD, dtype=jnp.int32)
    sent = project(order, parts, w_all, 1, jnp.bfloat16)
    arrived = lax.ppermute(sent, "p", SWAP)
    kept = project(order, parts, w_all, 0, jnp.float32)
    return (kept + arrived.astype(jnp.float32)).astype(jnp.bfloat16)


def solution(mesh):
    fine = Mesh(mesh.devices.reshape(SIZES), NAMES)
    return jax.shard_map(
        body,
        mesh=fine,
        in_specs=(P(CTX, HEAD), P(CTX, HEAD), P(CTX, HEAD), P(), P(HEAD, CTX)),
        out_specs=P(CTX, HEAD),
        check_vma=False,
    )
```

```python
import functools

import jax
import jax.numpy as jnp
from jax import lax
from jax.experimental import pallas as pl
from jax.experimental.pallas import tpu as pltpu
from jax.sharding import Mesh, PartitionSpec as P

HEAD_DIM = 128
ROUNDS = 2
SIZES = (2, 4, 4, 2, 2, 4)
NAMES = ("zh", "x", "y", "c", "p", "q")
CTX = ("zh", "x", "y", "c")
HEAD = ("p", "q")
PLANE = ("x", "y", "c")
SWAP = ((0, 1), (1, 0))
QUAD = 4
HALVES = 2
HINT_FLOPS, FIRST = 180 * 10**9, 20
PIECE = 16


def project_kernel(order_ref, *refs, side):
    parts, (w_ref, out_ref, held, arrivals) = refs[:QUAD], refs[QUAD:]
    width = w_ref.shape[-1]
    copies = [
        pltpu.make_async_copy(w_ref.at[order_ref[k], :, side], held.at[k], arrivals.at[k])
        for k in range(QUAD)
    ]
    for copy in copies:
        copy.start()
    total = 0.0
    for k in range(QUAD):
        copies[k].wait()
        total += lax.dot_general(
            parts[k][...],
            held[k].reshape(-1, width),
            (((1,), (1,)), ((), ())),
            preferred_element_type=jnp.float32,
        )
    out_ref[...] = total.astype(out_ref.dtype)


def project(order, parts, w_all, side, dtype):
    tokens, width = parts[0].shape
    _, chunks, _, columns, _ = w_all.shape
    in_vmem = pl.BlockSpec(memory_space=pltpu.VMEM)
    return pl.pallas_call(
        functools.partial(project_kernel, side=side),
        in_specs=[pl.BlockSpec(memory_space=pltpu.SMEM)]
        + [in_vmem] * QUAD
        + [pl.BlockSpec(memory_space=pltpu.HBM)],
        out_specs=in_vmem,
        out_shape=jax.ShapeDtypeStruct((tokens, chunks * columns), dtype),
        scratch_shapes=[
            pltpu.VMEM((QUAD, chunks, columns, width), w_all.dtype),
            pltpu.SemaphoreType.DMA((QUAD,)),
        ],
        compiler_params=pltpu.CompilerParams(vmem_limit_bytes=32 << 20),
        cost_estimate=pl.CostEstimate(
            flops=2 * QUAD * tokens * width * chunks * columns,
            bytes_accessed=2 * QUAD * width * (chunks * columns + tokens),
            transcendentals=0,
        ),
    )(order, *parts, pltpu.with_memory_space_constraint(w_all, pltpu.HBM))


def attend_kernel(own_ref, routed_ref, out_ref):
    _, tokens, width = own_ref.shape
    part = width // HALVES
    for head in range(width // HEAD_DIM):
        cols = slice(head * HEAD_DIM, (head + 1) * HEAD_DIM)
        at, lane = divmod(head * HEAD_DIM, part)

        def rows(kind, turn):
            piece = routed_ref[kind * HALVES + at, :, turn, :, lane : lane + HEAD_DIM]
            return piece.reshape(tokens, HEAD_DIM)

        query = own_ref[0, :, cols]
        scores = [
            lax.dot_general(
                query, keys, (((1,), (1,)), ((), ())), preferred_element_type=jnp.float32
            )
            * (1.0 / HEAD_DIM**0.5)
            for keys in [own_ref[1, :, cols]] + [rows(0, turn) for turn in range(ROUNDS)]
        ]
        peak = functools.reduce(jnp.maximum, scores)
        peak = jnp.max(peak, axis=-1, keepdims=True)
        exponents = [jnp.exp(score - peak) for score in scores]
        row_total = jnp.sum(functools.reduce(jnp.add, exponents), axis=-1, keepdims=True)
        summed = 0.0
        for exponent, values in zip(
            exponents, [own_ref[2, :, cols]] + [rows(1, turn) for turn in range(ROUNDS)]
        ):
            summed += jnp.dot(
                exponent.astype(jnp.bfloat16), values, preferred_element_type=jnp.float32
            )
        out_ref[:, cols] = (summed / row_total).astype(out_ref.dtype)


def attend(own, routed):
    _, tokens, width = own.shape
    in_vmem = pl.BlockSpec(memory_space=pltpu.VMEM)
    return pl.pallas_call(
        attend_kernel,
        in_specs=[in_vmem] * 2,
        out_specs=in_vmem,
        out_shape=jax.ShapeDtypeStruct((tokens, width), own.dtype),
        compiler_params=pltpu.CompilerParams(vmem_limit_bytes=32 << 20),
        cost_estimate=pl.CostEstimate(flops=HINT_FLOPS, bytes_accessed=10**6, transcendentals=0),
    )(own, routed)


def body(queries, keys, values, plan, w_out):
    tokens, width = queries.shape
    half = lax.axis_index("zh")
    quad, member = lax.axis_index("p"), lax.axis_index("q")
    seats = lax.axis_size(PLANE)

    w_near = lax.ppermute(
        w_out.T,
        ("x", "q"),
        [(x * QUAD + q, q * QUAD + x) for x in range(QUAD) for q in range(QUAD)],
    )

    part = width // HALVES
    own = jnp.stack(
        [rows[:, h * part : (h + 1) * part] for rows in (keys, values) for h in range(HALVES)]
    )
    own = own.reshape(seats, PIECE, part)
    spread = lax.all_to_all(own, PLANE, split_axis=0, concat_axis=0, tiled=True)
    spread, w_near = lax.optimization_barrier((spread, w_near))

    w_far = lax.ppermute(w_near, "zh", SWAP)
    keeps_near = half == quad
    w_pair = jnp.stack(
        (jnp.where(keeps_near, w_near, w_far), jnp.where(keeps_near, w_far, w_near))
    )
    spread = jnp.split(spread, (FIRST,))
    far = [lax.ppermute(spread[0], "zh", SWAP)]
    spread[1], w_pair = lax.optimization_barrier((spread[1], w_pair))
    far.append(lax.ppermute(spread[1], "zh", SWAP))
    w_all = lax.all_gather(w_pair, PLANE, axis=0, tiled=False)
    w_all = w_all.reshape(QUAD, seats // QUAD, 2, -1, width)

    block = jnp.stack((queries, keys, values))
    far, block = lax.optimization_barrier((far, block))

    wanted = lax.dynamic_slice_in_dim(plan, half * seats, seats, 1)
    place = (wanted // seats ^ half) * seats + wanted % seats
    chosen = jnp.concatenate((*spread, *far)).at[place.T].get(mode="promise_in_bounds")
    routed = lax.all_to_all(chosen, PLANE, split_axis=0, concat_axis=0, tiled=True)
    attended = attend(
        block, routed.reshape(2 * HALVES, tokens // PIECE, ROUNDS, PIECE, part)
    )

    parts = [attended] + [
        lax.ppermute(attended, "q", [(i, i ^ k) for i in range(QUAD)]) for k in range(1, QUAD)
    ]
    order = member ^ jnp.arange(QUAD, dtype=jnp.int32)
    sent = project(order, parts, w_all, 1, jnp.bfloat16)
    arrived = lax.ppermute(sent, "p", SWAP)
    kept = project(order, parts, w_all, 0, jnp.float32)
    return (kept + arrived.astype(jnp.float32)).astype(jnp.bfloat16)


def solution(mesh):
    fine = Mesh(mesh.devices.reshape(SIZES), NAMES)
    return jax.shard_map(
        body,
        mesh=fine,
        in_specs=(P(CTX, HEAD), P(CTX, HEAD), P(CTX, HEAD), P(), P(HEAD, CTX)),
        out_specs=P(CTX, HEAD),
        check_vma=False,
    )
```

```python
import functools

import jax
import jax.numpy as jnp
from jax import lax
from jax.experimental import pallas as pl
from jax.experimental.pallas import tpu as pltpu
from jax.sharding import Mesh, PartitionSpec as P

HEAD_DIM = 128
ROUNDS = 2
SIZES = (2, 4, 4, 2, 2, 4)
NAMES = ("zh", "x", "y", "c", "p", "q")
CTX = ("zh", "x", "y", "c")
HEAD = ("p", "q")
PLANE = ("x", "y", "c")
SWAP = ((0, 1), (1, 0))
QUAD = 4
HALVES = 2
PIECE = 16


def project_kernel(order_ref, *refs, side):
    parts, (w_ref, out_ref, held, arrivals) = refs[:QUAD], refs[QUAD:]
    width = w_ref.shape[-1]
    copies = [
        pltpu.make_async_copy(w_ref.at[order_ref[k], :, side], held.at[k], arrivals.at[k])
        for k in range(QUAD)
    ]
    for copy in copies:
        copy.start()
    total = 0.0
    for k in range(QUAD):
        copies[k].wait()
        total += lax.dot_general(
            parts[k][...],
            held[k].reshape(-1, width),
            (((1,), (1,)), ((), ())),
            preferred_element_type=jnp.float32,
        )
    out_ref[...] = total.astype(out_ref.dtype)


def project(order, parts, w_all, side, dtype):
    tokens, width = parts[0].shape
    _, chunks, _, columns, _ = w_all.shape
    in_vmem = pl.BlockSpec(memory_space=pltpu.VMEM)
    return pl.pallas_call(
        functools.partial(project_kernel, side=side),
        in_specs=[pl.BlockSpec(memory_space=pltpu.SMEM)]
        + [in_vmem] * QUAD
        + [pl.BlockSpec(memory_space=pltpu.HBM)],
        out_specs=in_vmem,
        out_shape=jax.ShapeDtypeStruct((tokens, chunks * columns), dtype),
        scratch_shapes=[
            pltpu.VMEM((QUAD, chunks, columns, width), w_all.dtype),
            pltpu.SemaphoreType.DMA((QUAD,)),
        ],
        compiler_params=pltpu.CompilerParams(vmem_limit_bytes=32 << 20),
        cost_estimate=pl.CostEstimate(
            flops=2 * QUAD * tokens * width * chunks * columns,
            bytes_accessed=2 * QUAD * width * (chunks * columns + tokens),
            transcendentals=0,
        ),
    )(order, *parts, pltpu.with_memory_space_constraint(w_all, pltpu.HBM))


def cut_kernel(keys_ref, values_ref, out_ref, arrivals):
    part = out_ref.shape[-1]
    copies = [
        pltpu.make_async_copy(
            rows.at[:, pl.ds(h * part, part)],
            out_ref.at[kind * HALVES + h],
            arrivals.at[kind, h],
        )
        for kind, rows in enumerate((keys_ref, values_ref))
        for h in range(HALVES)
    ]
    for copy in copies:
        copy.start()
    for copy in copies:
        copy.wait()


def cut(keys, values):
    tokens, width = keys.shape
    return pl.pallas_call(
        cut_kernel,
        in_specs=[pl.BlockSpec(memory_space=pltpu.HBM)] * 2,
        out_specs=pl.BlockSpec(memory_space=pltpu.VMEM),
        out_shape=jax.ShapeDtypeStruct((2 * HALVES, tokens, width // HALVES), keys.dtype),
        scratch_shapes=[pltpu.SemaphoreType.DMA((2, HALVES))],
        compiler_params=pltpu.CompilerParams(vmem_limit_bytes=16 << 20),
        cost_estimate=pl.CostEstimate(
            flops=0, bytes_accessed=8 * tokens * width, transcendentals=0
        ),
    )(
        *[pltpu.with_memory_space_constraint(rows, pltpu.HBM) for rows in (keys, values)],
    )


def attend_kernel(own_ref, routed_ref, out_ref):
    _, tokens, width = own_ref.shape
    part = width // HALVES
    for head in range(width // HEAD_DIM):
        cols = slice(head * HEAD_DIM, (head + 1) * HEAD_DIM)
        at, lane = divmod(head * HEAD_DIM, part)

        def rows(kind, turn):
            piece = routed_ref[kind * HALVES + at, :, turn, :, lane : lane + HEAD_DIM]
            return piece.reshape(tokens, HEAD_DIM)

        query = own_ref[0, :, cols]
        scores = [
            lax.dot_general(
                query, keys, (((1,), (1,)), ((), ())), preferred_element_type=jnp.float32
            )
            * (1.0 / HEAD_DIM**0.5)
            for keys in [own_ref[1, :, cols]] + [rows(0, turn) for turn in range(ROUNDS)]
        ]
        peak = functools.reduce(jnp.maximum, scores)
        peak = jnp.max(peak, axis=-1, keepdims=True)
        exponents = [jnp.exp(score - peak) for score in scores]
        row_total = jnp.sum(functools.reduce(jnp.add, exponents), axis=-1, keepdims=True)
        summed = 0.0
        for exponent, values in zip(
            exponents, [own_ref[2, :, cols]] + [rows(1, turn) for turn in range(ROUNDS)]
        ):
            summed += jnp.dot(
                exponent.astype(jnp.bfloat16), values, preferred_element_type=jnp.float32
            )
        out_ref[:, cols] = (summed / row_total).astype(out_ref.dtype)


def attend(own, routed):
    _, tokens, width = own.shape
    in_vmem = pl.BlockSpec(memory_space=pltpu.VMEM)
    return pl.pallas_call(
        attend_kernel,
        in_specs=[in_vmem] * 2,
        out_specs=in_vmem,
        out_shape=jax.ShapeDtypeStruct((tokens, width), own.dtype),
        compiler_params=pltpu.CompilerParams(vmem_limit_bytes=32 << 20),
        cost_estimate=pl.CostEstimate(
            flops=4 * tokens * width * (1 + ROUNDS) * tokens,
            bytes_accessed=2 * (own.size + routed.size + tokens * width),
            transcendentals=tokens * width * (1 + ROUNDS),
        ),
    )(own, routed)


def body(queries, keys, values, plan, w_out):
    tokens, width = queries.shape
    half = lax.axis_index("zh")
    quad, member = lax.axis_index("p"), lax.axis_index("q")
    seats = lax.axis_size(PLANE)

    w_near = lax.ppermute(
        w_out.T,
        ("x", "q"),
        [(x * QUAD + q, q * QUAD + x) for x in range(QUAD) for q in range(QUAD)],
    )

    part = width // HALVES
    own = cut(keys, values).reshape(seats, PIECE, part)
    spread = lax.all_to_all(own, PLANE, split_axis=0, concat_axis=0, tiled=True)
    spread, w_near = lax.optimization_barrier((spread, w_near))

    w_far = lax.ppermute(w_near, "zh", SWAP)
    far = lax.ppermute(spread, "zh", SWAP)
    keeps_near = half == quad
    w_pair = jnp.stack(
        (jnp.where(keeps_near, w_near, w_far), jnp.where(keeps_near, w_far, w_near))
    )
    w_all = lax.all_gather(w_pair, PLANE, axis=0, tiled=False)
    w_all = w_all.reshape(QUAD, seats // QUAD, 2, -1, width)

    block = jnp.stack((queries, keys, values))
    far, block = lax.optimization_barrier((far, block))

    wanted = lax.dynamic_slice_in_dim(plan, half * seats, seats, 1)
    place = (wanted // seats ^ half) * seats + wanted % seats
    chosen = jnp.concatenate((spread, far)).at[place.T].get(mode="promise_in_bounds")
    routed = lax.all_to_all(chosen, PLANE, split_axis=0, concat_axis=0, tiled=True)
    attended = attend(
        block, routed.reshape(2 * HALVES, tokens // PIECE, ROUNDS, PIECE, part)
    )

    parts = [attended] + [
        lax.ppermute(attended, "q", [(i, i ^ k) for i in range(QUAD)]) for k in range(1, QUAD)
    ]
    order = member ^ jnp.arange(QUAD, dtype=jnp.int32)
    sent = project(order, parts, w_all, 1, jnp.bfloat16)
    arrived = lax.ppermute(sent, "p", SWAP)
    kept = project(order, parts, w_all, 0, jnp.float32)
    return (kept + arrived.astype(jnp.float32)).astype(jnp.bfloat16)


def solution(mesh):
    fine = Mesh(mesh.devices.reshape(SIZES), NAMES)
    return jax.shard_map(
        body,
        mesh=fine,
        in_specs=(P(CTX, HEAD), P(CTX, HEAD), P(CTX, HEAD), P(), P(HEAD, CTX)),
        out_specs=P(CTX, HEAD),
        check_vma=False,
    )
```

```python
import functools

import jax
import jax.numpy as jnp
from jax import lax
from jax.experimental import pallas as pl
from jax.experimental.pallas import tpu as pltpu
from jax.sharding import Mesh, PartitionSpec as P

HEAD_DIM = 128
ROUNDS = 2
SIZES = (2, 4, 4, 2, 2, 4)
NAMES = ("zh", "x", "y", "c", "p", "q")
CTX = ("zh", "x", "y", "c")
HEAD = ("p", "q")
PLANE = ("x", "y", "c")
SWAP = ((0, 1), (1, 0))
QUAD = 4
HALVES = 2
PIECE = 16


def project_kernel(order_ref, *refs, side, first):
    parts, (w_ref, out_ref, held, arrivals) = refs[:QUAD], refs[QUAD:]
    width = w_ref.shape[-1]
    copies = [
        pltpu.make_async_copy(
            w_ref.at[order_ref[k], pl.ds(first, held.shape[1]), side], held.at[k], arrivals.at[k]
        )
        for k in range(QUAD)
    ]
    for copy in copies:
        copy.start()
    total = 0.0
    for k in range(QUAD):
        copies[k].wait()
        total += lax.dot_general(
            parts[k][...],
            held[k].reshape(-1, width),
            (((1,), (1,)), ((), ())),
            preferred_element_type=jnp.float32,
        )
    out_ref[...] = total.astype(out_ref.dtype)


def project(order, parts, w_all, side, dtype, first=0, chunks=None):
    tokens, width = parts[0].shape
    columns = w_all.shape[3]
    chunks = chunks or w_all.shape[1]
    in_vmem = pl.BlockSpec(memory_space=pltpu.VMEM)
    return pl.pallas_call(
        functools.partial(project_kernel, side=side, first=first),
        in_specs=[pl.BlockSpec(memory_space=pltpu.SMEM)]
        + [in_vmem] * QUAD
        + [pl.BlockSpec(memory_space=pltpu.HBM)],
        out_specs=in_vmem,
        out_shape=jax.ShapeDtypeStruct((tokens, chunks * columns), dtype),
        scratch_shapes=[
            pltpu.VMEM((QUAD, chunks, columns, width), w_all.dtype),
            pltpu.SemaphoreType.DMA((QUAD,)),
        ],
        compiler_params=pltpu.CompilerParams(vmem_limit_bytes=32 << 20),
        cost_estimate=pl.CostEstimate(
            flops=2 * QUAD * tokens * width * chunks * columns,
            bytes_accessed=2 * QUAD * width * (chunks * columns + tokens),
            transcendentals=0,
        ),
    )(order, *parts, pltpu.with_memory_space_constraint(w_all, pltpu.HBM))


def cut_kernel(keys_ref, values_ref, out_ref, arrivals):
    part = out_ref.shape[-1]
    copies = [
        pltpu.make_async_copy(
            rows.at[:, pl.ds(h * part, part)],
            out_ref.at[kind * HALVES + h],
            arrivals.at[kind, h],
        )
        for kind, rows in enumerate((keys_ref, values_ref))
        for h in range(HALVES)
    ]
    for copy in copies:
        copy.start()
    for copy in copies:
        copy.wait()


def cut(keys, values):
    tokens, width = keys.shape
    return pl.pallas_call(
        cut_kernel,
        in_specs=[pl.BlockSpec(memory_space=pltpu.HBM)] * 2,
        out_specs=pl.BlockSpec(memory_space=pltpu.VMEM),
        out_shape=jax.ShapeDtypeStruct((2 * HALVES, tokens, width // HALVES), keys.dtype),
        scratch_shapes=[pltpu.SemaphoreType.DMA((2, HALVES))],
        compiler_params=pltpu.CompilerParams(vmem_limit_bytes=16 << 20),
        cost_estimate=pl.CostEstimate(
            flops=0, bytes_accessed=8 * tokens * width, transcendentals=0
        ),
    )(
        *[pltpu.with_memory_space_constraint(rows, pltpu.HBM) for rows in (keys, values)],
    )


def attend_kernel(own_ref, routed_ref, out_ref):
    _, tokens, width = own_ref.shape
    part = width // HALVES
    for head in range(width // HEAD_DIM):
        cols = slice(head * HEAD_DIM, (head + 1) * HEAD_DIM)
        at, lane = divmod(head * HEAD_DIM, part)

        def rows(kind, turn):
            piece = routed_ref[kind * HALVES + at, :, turn, :, lane : lane + HEAD_DIM]
            return piece.reshape(tokens, HEAD_DIM)

        query = own_ref[0, :, cols]
        scores = [
            lax.dot_general(
                query, keys, (((1,), (1,)), ((), ())), preferred_element_type=jnp.float32
            )
            * (1.0 / HEAD_DIM**0.5)
            for keys in [own_ref[1, :, cols]] + [rows(0, turn) for turn in range(ROUNDS)]
        ]
        peak = functools.reduce(jnp.maximum, scores)
        peak = jnp.max(peak, axis=-1, keepdims=True)
        exponents = [jnp.exp(score - peak) for score in scores]
        row_total = jnp.sum(functools.reduce(jnp.add, exponents), axis=-1, keepdims=True)
        summed = 0.0
        for exponent, values in zip(
            exponents, [own_ref[2, :, cols]] + [rows(1, turn) for turn in range(ROUNDS)]
        ):
            summed += jnp.dot(
                exponent.astype(jnp.bfloat16), values, preferred_element_type=jnp.float32
            )
        out_ref[:, cols] = (summed / row_total).astype(out_ref.dtype)


def attend(own, routed):
    _, tokens, width = own.shape
    in_vmem = pl.BlockSpec(memory_space=pltpu.VMEM)
    return pl.pallas_call(
        attend_kernel,
        in_specs=[in_vmem] * 2,
        out_specs=in_vmem,
        out_shape=jax.ShapeDtypeStruct((tokens, width), own.dtype),
        compiler_params=pltpu.CompilerParams(vmem_limit_bytes=32 << 20),
        cost_estimate=pl.CostEstimate(
            flops=4 * tokens * width * (1 + ROUNDS) * tokens,
            bytes_accessed=2 * (own.size + routed.size + tokens * width),
            transcendentals=tokens * width * (1 + ROUNDS),
        ),
    )(own, routed)


def body(queries, keys, values, plan, w_out):
    tokens, width = queries.shape
    half = lax.axis_index("zh")
    quad, member = lax.axis_index("p"), lax.axis_index("q")
    seats = lax.axis_size(PLANE)

    w_near = lax.ppermute(
        w_out.T,
        ("x", "q"),
        [(x * QUAD + q, q * QUAD + x) for x in range(QUAD) for q in range(QUAD)],
    )

    part = width // HALVES
    own = cut(keys, values).reshape(seats, PIECE, part)
    spread = lax.all_to_all(own, PLANE, split_axis=0, concat_axis=0, tiled=True)
    spread, w_near = lax.optimization_barrier((spread, w_near))

    w_far = lax.ppermute(w_near, "zh", SWAP)
    far = lax.ppermute(spread, "zh", SWAP)
    keeps_near = half == quad
    w_pair = jnp.stack(
        (jnp.where(keeps_near, w_near, w_far), jnp.where(keeps_near, w_far, w_near))
    )
    w_all = lax.all_gather(w_pair, PLANE, axis=0, tiled=False)
    w_all = w_all.reshape(QUAD, seats // QUAD, 2, -1, width)

    block = jnp.stack((queries, keys, values))
    far, block = lax.optimization_barrier((far, block))

    wanted = lax.dynamic_slice_in_dim(plan, half * seats, seats, 1)
    place = (wanted // seats ^ half) * seats + wanted % seats
    chosen = jnp.concatenate((spread, far)).at[place.T].get(mode="promise_in_bounds")
    routed = lax.all_to_all(chosen, PLANE, split_axis=0, concat_axis=0, tiled=True)
    attended = attend(
        block, routed.reshape(2 * HALVES, tokens // PIECE, ROUNDS, PIECE, part)
    )

    steps = (0, 2, 3, 1)
    parts = [attended] + [
        lax.ppermute(attended, "q", [(i, i ^ k) for i in range(QUAD)]) for k in steps[1:]
    ]
    order = member ^ jnp.array(steps, jnp.int32)
    chunks = w_all.shape[1] // 2
    arrived = [
        lax.ppermute(
            project(order, parts, w_all, 1, jnp.bfloat16, h * chunks, chunks), "p", SWAP
        )
        for h in range(2)
    ]
    arrived = jnp.concatenate(arrived, 1)
    kept = project(order, parts, w_all, 0, jnp.float32)
    return (kept + arrived.astype(jnp.float32)).astype(jnp.bfloat16)


def solution(mesh):
    fine = Mesh(mesh.devices.reshape(SIZES), NAMES)
    return jax.shard_map(
        body,
        mesh=fine,
        in_specs=(P(CTX, HEAD), P(CTX, HEAD), P(CTX, HEAD), P(), P(HEAD, CTX)),
        out_specs=P(CTX, HEAD),
        check_vma=False,
    )
```

```python
import functools

import jax
import jax.numpy as jnp
from jax import lax
from jax.experimental import pallas as pl
from jax.experimental.pallas import tpu as pltpu
from jax.sharding import Mesh, PartitionSpec as P

HEAD_DIM = 128
ROUNDS = 2
SIZES = (2, 4, 4, 2, 2, 4)
NAMES = ("zh", "x", "y", "c", "p", "q")
CTX = ("zh", "x", "y", "c")
HEAD = ("p", "q")
PLANE = ("x", "y", "c")
SWAP = ((0, 1), (1, 0))
QUAD = 4
HALVES = 2
PIECE = 16


def project_kernel(order_ref, *refs, side):
    parts, (w_ref, out_ref, held, arrivals) = refs[:QUAD], refs[QUAD:]
    width = w_ref.shape[-1]
    copies = [
        pltpu.make_async_copy(w_ref.at[order_ref[k], :, side], held.at[k], arrivals.at[k])
        for k in range(QUAD)
    ]
    copies[0].start()
    copies[1].start()
    total = 0.0
    for k in range(QUAD):
        copies[k].wait()
        if k + 2 < QUAD:
            copies[k + 2].start()
        total += lax.dot_general(
            parts[k][...],
            held[k].reshape(-1, width),
            (((1,), (1,)), ((), ())),
            preferred_element_type=jnp.float32,
        )
    out_ref[...] = total.astype(out_ref.dtype)


def project(order, parts, w_all, side, dtype):
    tokens, width = parts[0].shape
    _, chunks, _, columns, _ = w_all.shape
    in_vmem = pl.BlockSpec(memory_space=pltpu.VMEM)
    return pl.pallas_call(
        functools.partial(project_kernel, side=side),
        in_specs=[pl.BlockSpec(memory_space=pltpu.SMEM)]
        + [in_vmem] * QUAD
        + [pl.BlockSpec(memory_space=pltpu.HBM)],
        out_specs=in_vmem,
        out_shape=jax.ShapeDtypeStruct((tokens, chunks * columns), dtype),
        scratch_shapes=[
            pltpu.VMEM((QUAD, chunks, columns, width), w_all.dtype),
            pltpu.SemaphoreType.DMA((QUAD,)),
        ],
        compiler_params=pltpu.CompilerParams(vmem_limit_bytes=32 << 20),
        cost_estimate=pl.CostEstimate(
            flops=2 * QUAD * tokens * width * chunks * columns,
            bytes_accessed=2 * QUAD * width * (chunks * columns + tokens),
            transcendentals=0,
        ),
    )(order, *parts, pltpu.with_memory_space_constraint(w_all, pltpu.HBM))


def cut_kernel(keys_ref, values_ref, out_ref, arrivals):
    part = out_ref.shape[-1]
    copies = [
        pltpu.make_async_copy(
            rows.at[:, pl.ds(h * part, part)],
            out_ref.at[kind * HALVES + h],
            arrivals.at[kind, h],
        )
        for kind, rows in enumerate((keys_ref, values_ref))
        for h in range(HALVES)
    ]
    for copy in copies:
        copy.start()
    for copy in copies:
        copy.wait()


def cut(keys, values):
    tokens, width = keys.shape
    return pl.pallas_call(
        cut_kernel,
        in_specs=[pl.BlockSpec(memory_space=pltpu.HBM)] * 2,
        out_specs=pl.BlockSpec(memory_space=pltpu.VMEM),
        out_shape=jax.ShapeDtypeStruct((2 * HALVES, tokens, width // HALVES), keys.dtype),
        scratch_shapes=[pltpu.SemaphoreType.DMA((2, HALVES))],
        compiler_params=pltpu.CompilerParams(vmem_limit_bytes=16 << 20),
        cost_estimate=pl.CostEstimate(
            flops=0, bytes_accessed=8 * tokens * width, transcendentals=0
        ),
    )(
        *[pltpu.with_memory_space_constraint(rows, pltpu.HBM) for rows in (keys, values)],
    )


def attend_kernel(own_ref, routed_ref, out_ref):
    _, tokens, width = own_ref.shape
    part = width // HALVES
    for head in range(width // HEAD_DIM):
        cols = slice(head * HEAD_DIM, (head + 1) * HEAD_DIM)
        at, lane = divmod(head * HEAD_DIM, part)

        def rows(kind, turn):
            piece = routed_ref[kind * HALVES + at, :, turn, :, lane : lane + HEAD_DIM]
            return piece.reshape(tokens, HEAD_DIM)

        query = own_ref[0, :, cols]
        scores = [
            lax.dot_general(
                query, keys, (((1,), (1,)), ((), ())), preferred_element_type=jnp.float32
            )
            * (1.0 / HEAD_DIM**0.5)
            for keys in [own_ref[1, :, cols]] + [rows(0, turn) for turn in range(ROUNDS)]
        ]
        peak = functools.reduce(jnp.maximum, scores)
        peak = jnp.max(peak, axis=-1, keepdims=True)
        exponents = [jnp.exp(score - peak) for score in scores]
        row_total = jnp.sum(functools.reduce(jnp.add, exponents), axis=-1, keepdims=True)
        summed = 0.0
        for exponent, values in zip(
            exponents, [own_ref[2, :, cols]] + [rows(1, turn) for turn in range(ROUNDS)]
        ):
            summed += jnp.dot(
                exponent.astype(jnp.bfloat16), values, preferred_element_type=jnp.float32
            )
        out_ref[:, cols] = (summed / row_total).astype(out_ref.dtype)


def attend(own, routed):
    _, tokens, width = own.shape
    in_vmem = pl.BlockSpec(memory_space=pltpu.VMEM)
    return pl.pallas_call(
        attend_kernel,
        in_specs=[in_vmem] * 2,
        out_specs=in_vmem,
        out_shape=jax.ShapeDtypeStruct((tokens, width), own.dtype),
        compiler_params=pltpu.CompilerParams(vmem_limit_bytes=32 << 20),
        cost_estimate=pl.CostEstimate(
            flops=4 * tokens * width * (1 + ROUNDS) * tokens,
            bytes_accessed=2 * (own.size + routed.size + tokens * width),
            transcendentals=tokens * width * (1 + ROUNDS),
        ),
    )(own, routed)


def body(queries, keys, values, plan, w_out):
    tokens, width = queries.shape
    half = lax.axis_index("zh")
    quad, member = lax.axis_index("p"), lax.axis_index("q")
    seats = lax.axis_size(PLANE)

    w_near = lax.ppermute(
        w_out.T,
        ("x", "q"),
        [(x * QUAD + q, q * QUAD + x) for x in range(QUAD) for q in range(QUAD)],
    )

    part = width // HALVES
    own = cut(keys, values).reshape(seats, PIECE, part)
    spread = lax.all_to_all(own, PLANE, split_axis=0, concat_axis=0, tiled=True)
    spread, w_near = lax.optimization_barrier((spread, w_near))

    w_far = lax.ppermute(w_near, "zh", SWAP)
    far = lax.ppermute(spread, "zh", SWAP)
    keeps_near = half == quad
    w_pair = jnp.stack(
        (jnp.where(keeps_near, w_near, w_far), jnp.where(keeps_near, w_far, w_near))
    )
    w_all = lax.all_gather(w_pair, PLANE, axis=0, tiled=False)
    w_all = w_all.reshape(QUAD, seats // QUAD, 2, -1, width)

    block = jnp.stack((queries, keys, values))
    far, block = lax.optimization_barrier((far, block))

    wanted = lax.dynamic_slice_in_dim(plan, half * seats, seats, 1)
    place = (wanted // seats ^ half) * seats + wanted % seats
    chosen = jnp.concatenate((spread, far)).at[place.T].get(mode="promise_in_bounds")
    routed = lax.all_to_all(chosen, PLANE, split_axis=0, concat_axis=0, tiled=True)
    attended = attend(
        block, routed.reshape(2 * HALVES, tokens // PIECE, ROUNDS, PIECE, part)
    )

    parts = [attended] + [
        lax.ppermute(attended, "q", [(i, i ^ k) for i in range(QUAD)]) for k in range(1, QUAD)
    ]
    order = member ^ jnp.arange(QUAD, dtype=jnp.int32)
    sent = project(order, parts, w_all, 1, jnp.bfloat16)
    arrived = lax.ppermute(sent, "p", SWAP)
    kept = project(order, parts, w_all, 0, jnp.float32)
    return (kept + arrived.astype(jnp.float32)).astype(jnp.bfloat16)


def solution(mesh):
    fine = Mesh(mesh.devices.reshape(SIZES), NAMES)
    return jax.shard_map(
        body,
        mesh=fine,
        in_specs=(P(CTX, HEAD), P(CTX, HEAD), P(CTX, HEAD), P(), P(HEAD, CTX)),
        out_specs=P(CTX, HEAD),
        check_vma=False,
    )
```

```python
import functools

import jax
import jax.numpy as jnp
from jax import lax
from jax.experimental import pallas as pl
from jax.experimental.pallas import tpu as pltpu
from jax.sharding import Mesh, PartitionSpec as P

HEAD_DIM = 128
ROUNDS = 2
SIZES = (2, 4, 4, 2, 2, 4)
NAMES = ("zh", "x", "y", "c", "p", "q")
CTX = ("zh", "x", "y", "c")
HEAD = ("p", "q")
PLANE = ("x", "y", "c")
SWAP = ((0, 1), (1, 0))
QUAD = 4
HALVES = 2
PIECE = 16


def project_kernel(order_ref, *refs, side):
    parts, (w_ref, out_ref, held, arrivals) = refs[:QUAD], refs[QUAD:]
    width = w_ref.shape[-1]
    copies = [
        pltpu.make_async_copy(w_ref.at[order_ref[k], :, side], held.at[k], arrivals.at[k])
        for k in range(QUAD)
    ]
    for copy in copies:
        copy.start()
    total = 0.0
    for k in range(QUAD):
        copies[k].wait()
        total += lax.dot_general(
            parts[k][...],
            held[k].reshape(-1, width),
            (((1,), (1,)), ((), ())),
            preferred_element_type=jnp.float32,
        )
    out_ref[...] = total.astype(out_ref.dtype)


def project(order, parts, w_all, side, dtype):
    tokens, width = parts[0].shape
    _, chunks, _, columns, _ = w_all.shape
    in_vmem = pl.BlockSpec(memory_space=pltpu.VMEM)
    return pl.pallas_call(
        functools.partial(project_kernel, side=side),
        in_specs=[pl.BlockSpec(memory_space=pltpu.SMEM)]
        + [in_vmem] * QUAD
        + [pl.BlockSpec(memory_space=pltpu.HBM)],
        out_specs=in_vmem,
        out_shape=jax.ShapeDtypeStruct((tokens, chunks * columns), dtype),
        scratch_shapes=[
            pltpu.VMEM((QUAD, chunks, columns, width), w_all.dtype),
            pltpu.SemaphoreType.DMA((QUAD,)),
        ],
        compiler_params=pltpu.CompilerParams(vmem_limit_bytes=32 << 20),
        cost_estimate=pl.CostEstimate(
            flops=2 * QUAD * tokens * width * chunks * columns,
            bytes_accessed=2 * QUAD * width * (chunks * columns + tokens),
            transcendentals=0,
        ),
    )(order, *parts, pltpu.with_memory_space_constraint(w_all, pltpu.HBM))


def cut_kernel(keys_ref, values_ref, out_ref, arrivals):
    part = out_ref.shape[-1]
    copies = [
        pltpu.make_async_copy(
            rows.at[:, pl.ds(h * part, part)],
            out_ref.at[kind * HALVES + h],
            arrivals.at[kind, h],
        )
        for kind, rows in enumerate((keys_ref, values_ref))
        for h in range(HALVES)
    ]
    for copy in copies:
        copy.start()
    for copy in copies:
        copy.wait()


def cut(keys, values):
    tokens, width = keys.shape
    return pl.pallas_call(
        cut_kernel,
        in_specs=[pl.BlockSpec(memory_space=pltpu.HBM)] * 2,
        out_specs=pl.BlockSpec(memory_space=pltpu.VMEM),
        out_shape=jax.ShapeDtypeStruct((2 * HALVES, tokens, width // HALVES), keys.dtype),
        scratch_shapes=[pltpu.SemaphoreType.DMA((2, HALVES))],
        compiler_params=pltpu.CompilerParams(vmem_limit_bytes=16 << 20),
        cost_estimate=pl.CostEstimate(
            flops=0, bytes_accessed=8 * tokens * width, transcendentals=0
        ),
    )(
        *[pltpu.with_memory_space_constraint(rows, pltpu.HBM) for rows in (keys, values)],
    )


def attend_kernel(own_ref, routed_ref, out_ref):
    _, tokens, width = own_ref.shape
    part = width // HALVES
    for head in range(width // HEAD_DIM):
        cols = slice(head * HEAD_DIM, (head + 1) * HEAD_DIM)
        at, lane = divmod(head * HEAD_DIM, part)

        def rows(kind, turn):
            piece = routed_ref[kind * HALVES + at, :, turn, :, lane : lane + HEAD_DIM]
            return piece.reshape(tokens, HEAD_DIM)

        keys, values = [
            jnp.concatenate(
                [own_ref[1 + kind, :, cols]] + [rows(kind, turn) for turn in range(ROUNDS)]
            )
            for kind in range(2)
        ]
        scores = lax.dot_general(
            own_ref[0, :, cols], keys, (((1,), (1,)), ((), ())), preferred_element_type=jnp.float32
        ) * (1.0 / HEAD_DIM**0.5)
        exponent = jnp.exp(scores - jnp.max(scores, axis=-1, keepdims=True))
        row_total = jnp.sum(exponent, axis=-1, keepdims=True)
        summed = jnp.dot(
            exponent.astype(jnp.bfloat16), values, preferred_element_type=jnp.float32
        )
        out_ref[:, cols] = (summed / row_total).astype(out_ref.dtype)


def attend(own, routed):
    _, tokens, width = own.shape
    in_vmem = pl.BlockSpec(memory_space=pltpu.VMEM)
    return pl.pallas_call(
        attend_kernel,
        in_specs=[in_vmem] * 2,
        out_specs=in_vmem,
        out_shape=jax.ShapeDtypeStruct((tokens, width), own.dtype),
        compiler_params=pltpu.CompilerParams(vmem_limit_bytes=32 << 20),
        cost_estimate=pl.CostEstimate(
            flops=4 * tokens * width * (1 + ROUNDS) * tokens,
            bytes_accessed=2 * (own.size + routed.size + tokens * width),
            transcendentals=tokens * width * (1 + ROUNDS),
        ),
    )(own, routed)


def body(queries, keys, values, plan, w_out):
    tokens, width = queries.shape
    half = lax.axis_index("zh")
    quad, member = lax.axis_index("p"), lax.axis_index("q")
    seats = lax.axis_size(PLANE)

    w_near = lax.ppermute(
        w_out.T,
        ("x", "q"),
        [(x * QUAD + q, q * QUAD + x) for x in range(QUAD) for q in range(QUAD)],
    )

    part = width // HALVES
    own = cut(keys, values).reshape(seats, PIECE, part)
    spread = lax.all_to_all(own, PLANE, split_axis=0, concat_axis=0, tiled=True)
    spread, w_near = lax.optimization_barrier((spread, w_near))

    w_far = lax.ppermute(w_near, "zh", SWAP)
    far = lax.ppermute(spread, "zh", SWAP)
    keeps_near = half == quad
    w_pair = jnp.stack(
        (jnp.where(keeps_near, w_near, w_far), jnp.where(keeps_near, w_far, w_near))
    )
    w_all = lax.all_gather(w_pair, PLANE, axis=0, tiled=False)
    w_all = w_all.reshape(QUAD, seats // QUAD, 2, -1, width)

    block = jnp.stack((queries, keys, values))
    far, block = lax.optimization_barrier((far, block))

    wanted = lax.dynamic_slice_in_dim(plan, half * seats, seats, 1)
    place = (wanted // seats ^ half) * seats + wanted % seats
    chosen = jnp.concatenate((spread, far)).at[place.T].get(mode="promise_in_bounds")
    routed = lax.all_to_all(chosen, PLANE, split_axis=0, concat_axis=0, tiled=True)
    attended = attend(
        block, routed.reshape(2 * HALVES, tokens // PIECE, ROUNDS, PIECE, part)
    )

    parts = [attended] + [
        lax.ppermute(attended, "q", [(i, i ^ k) for i in range(QUAD)]) for k in range(1, QUAD)
    ]
    order = member ^ jnp.arange(QUAD, dtype=jnp.int32)
    sent = project(order, parts, w_all, 1, jnp.bfloat16)
    arrived = lax.ppermute(sent, "p", SWAP)
    kept = project(order, parts, w_all, 0, jnp.float32)
    return (kept + arrived.astype(jnp.float32)).astype(jnp.bfloat16)


def solution(mesh):
    fine = Mesh(mesh.devices.reshape(SIZES), NAMES)
    return jax.shard_map(
        body,
        mesh=fine,
        in_specs=(P(CTX, HEAD), P(CTX, HEAD), P(CTX, HEAD), P(), P(HEAD, CTX)),
        out_specs=P(CTX, HEAD),
        check_vma=False,
    )
```
